32 devices in a mesh: tm: 4 (over z), gx: 2 (over y), gy: 4 (over x, core).
Axes of the slice: x: 2, y: 2, z: 4, core: 2. Of those that a mesh axis runs over, the one named last changes fastest.
Arguments:
- fine_nodes: float32 [4, 3, 64, 256, 128], P('tm', None, 'gx', 'gy'), may hold values from -1 to 1
- section_steps: int32 [4], replicated, may hold values from 1 to 4
- diffusivities: float32 [16], replicated, may hold values from 0.5 to 4
- tile_kinds: int32 [16, 64], P('gx', 'gy'), may hold values from 0 to 15
Outputs:
- next_nodes: float32 [4, 3, 64, 256, 128], P('tm', None, 'gx', 'gy')
The draws below stay inside these ranges and needn't reach their ends.
All inputs are finite; a program needn't handle non-finite values.
Results may differ from the reference program's by a relative error of at most 0.0001.
Values sent between devices are 32-bit elements; how exact they have to be, the bound alone decides.
No kernel may reach another device: no remote copies, remote signals or barrier semaphores. Data moves between devices by JAX's collectives and lax.ppermute only.
A program may use at most 128 MiB of HBM per device.

```python
import math
import jax
import jax.numpy as jnp

CZ = 128
NODES = 3
JACOBI = 4
TILE = 4
KINDS = 16
SECTIONS = 4
NX = 64
NY = 256


def place_ends(values, key, smallest, top_value):
    longest = values.shape.index(max(values.shape))
    spots = []
    for shift in (0, 1):
        where = [jax.random.randint(jax.random.fold_in(key, axis), (), 0, length) for axis, length in enumerate(values.shape)]
        where[longest] = (where[longest] + shift) % values.shape[longest]
        spots.append(tuple(where))
    return values.at[spots[0]].set(smallest).at[spots[1]].set(top_value)


def level_of(own_key, dims, cuts, low, high):
    loudness, own = 1.0, jax.random.fold_in(own_key, 6)
    for dim, parts in cuts:
        draws = jnp.exp(jax.random.uniform(jax.random.fold_in(own, dim), (parts,), jnp.float32, low / len(cuts), high / len(cuts)))
        loudness = loudness * jnp.repeat(draws, dims[dim] // parts).reshape([-1 if axis == dim else 1 for axis in range(len(dims))])
    return loudness


def setup_inputs(seed: int = 0) -> dict:
    streams_of = jax.random.split(jax.random.key(seed), 5)
    return {
        "fine_nodes": jnp.clip(jax.random.uniform(streams_of[0], (SECTIONS, NODES, NX, NY, CZ), jnp.float32, -1.0, 1.0) * level_of(streams_of[0], (SECTIONS, NODES, NX, NY, CZ), ((0, 4), (2, 2), (3, 4)), -0.4, 0.0), -1.0, 1.0),
        "section_steps": place_ends(jax.random.randint(streams_of[1], (SECTIONS,), 1, 5), jax.random.fold_in(streams_of[1], 1), 1, 4).astype(jnp.int32),
        "diffusivities": jnp.clip(jnp.exp(jax.random.uniform(streams_of[2], (KINDS,), jnp.float32, math.log(0.5), math.log(4.0))), 0.5, 4.0),
        "tile_kinds": place_ends(jax.random.randint(streams_of[3], (NX // TILE, NY // TILE), 0, KINDS), jax.random.fold_in(streams_of[3], 1), 0, KINDS - 1).astype(jnp.int32),
    }


step_unit = 0.05
node_weights = ((5.0 / 24.0, 1.0 / 3.0, -1.0 / 24.0), (-1.0 / 24.0, 1.0 / 3.0, 5.0 / 24.0))


def shifted_sums(padded):
    center = padded[..., 1:-1, 1:-1, :]
    planar = padded[..., 2:, 1:-1, :] + padded[..., :-2, 1:-1, :]
    planar = planar + padded[..., 1:-1, 2:, :] + padded[..., 1:-1, :-2, :]
    zero_plane = jnp.zeros(center.shape[:-1] + (1,), center.dtype)
    z_above = jnp.concatenate([center[..., 1:], zero_plane], axis=-1)
    z_below = jnp.concatenate([zero_plane, center[..., :-1]], axis=-1)
    return center, planar, z_above + z_below


def reaction(field):
    return field - field * field * field


def forces_of(padded, diffusivity, planar_weight):
    center, planar, vertical = shifted_sums(padded)
    laplace = planar_weight * planar + vertical - (4.0 * planar_weight + 2.0) * center
    return reaction(center), diffusivity * laplace


def jacobi_update(padded, right_side, diffusivity, half_step, planar_weight):
    sums = shifted_sums(padded)
    coupling = half_step * diffusivity
    return (right_side + coupling * (planar_weight * sums[1] + sums[2])) / (1.0 + coupling * (4.0 * planar_weight + 2.0))


def restrict(field):
    shape = field.shape
    blocks = field.reshape(shape[:-3] + (shape[-3] // 2, 2, shape[-2] // 2, 2, shape[-1]))
    return (blocks[..., :, 0, :, 0, :] + blocks[..., :, 0, :, 1, :] + blocks[..., :, 1, :, 0, :] + blocks[..., :, 1, :, 1, :]) * 0.25


def prolong(field):
    return jnp.repeat(jnp.repeat(field, 2, axis=-3), 2, axis=-2)


def sweep(start_value, node_vals, reactions, diffusion, forces, tau_terms, half_step, step_size, diffusivity, planar_weight, solver):
    updated = [start_value]
    for node_num in range(len(node_weights)):
        weights = node_weights[node_num]
        integral = weights[0] * forces[0] + weights[1] * forces[1] + weights[2] * forces[2]
        right_side = updated[node_num] + half_step * (reaction(updated[node_num]) - reactions[node_num]) - half_step * diffusion[node_num + 1] + step_size * integral
        if tau_terms is not None:
            right_side = right_side + tau_terms[node_num]
        updated.append(solver(right_side, node_vals[node_num + 1], diffusivity, half_step, planar_weight))
    return jnp.stack(updated)


def pad_planes(field):
    return jnp.pad(field, [(0, 0)] * (field.ndim - 3) + [(1, 1), (1, 1), (0, 0)])


def whole_solver(right_side, initial, diffusivity, half_step, planar_weight):
    current = initial
    for iter_num in range(JACOBI):
        current = jacobi_update(pad_planes(current), right_side, diffusivity, half_step, planar_weight)
    return current


def reference(fine_nodes, section_steps, diffusivities, tile_kinds):
    tile_values = diffusivities[tile_kinds]
    diffusivity = jnp.repeat(jnp.repeat(tile_values, TILE, axis=0), TILE, axis=1)[:, :, None]
    coarse_diffusivity = restrict(diffusivity)
    step_sizes = section_steps.astype(jnp.float32) * step_unit
    outputs = []
    coarse_end = None
    fine_end = None
    for sect_num in range(SECTIONS):
        step_size = step_sizes[sect_num]
        half_step = step_size * 0.5
        node_vals = fine_nodes[sect_num]
        reactions, diffusion = forces_of(pad_planes(node_vals), diffusivity, 1.0)
        forces = reactions + diffusion
        updated = sweep(node_vals[0], node_vals, reactions, diffusion, forces, None, half_step, step_size, diffusivity, 1.0, whole_solver)
        late_react, late_diff = forces_of(pad_planes(updated[1:]), diffusivity, 1.0)
        fine_forces = jnp.concatenate([forces[:1], late_react + late_diff])
        coarse_nodes = restrict(updated)
        restricted = restrict(fine_forces)
        coarse_react, coarse_diff = forces_of(pad_planes(coarse_nodes), coarse_diffusivity, 0.25)
        coarse_forces = coarse_react + coarse_diff
        defect = restricted - coarse_forces
        tau_terms = jnp.stack([step_size * (weights[0] * defect[0] + weights[1] * defect[1] + weights[2] * defect[2]) for weights in node_weights])
        start_value = coarse_nodes[0] if sect_num == 0 else coarse_end
        chained = sweep(start_value, coarse_nodes, coarse_react, coarse_diff, coarse_forces, tau_terms, half_step, step_size, coarse_diffusivity, 0.25, whole_solver)
        coarse_end = chained[2]
        corrected = updated + prolong(chained - coarse_nodes)
        first = corrected[0] if sect_num == 0 else fine_end
        outputs.append(jnp.concatenate([first[None], corrected[1:]]))
        fine_end = corrected[2]
    return jnp.stack(outputs)
```

```python
import functools
import jax
import jax.numpy as jnp
from jax import lax
from jax.experimental import pallas as pl
from jax.experimental.pallas import tpu as pltpu
from jax.sharding import PartitionSpec as P

TILE = 4
FW = 8
CW = 6
CN = 3
YW = 8
STEP_UNIT = 0.05
WEIGHTS = ((5.0 / 24.0, 1.0 / 3.0, -1.0 / 24.0), (-1.0 / 24.0, 1.0 / 3.0, 5.0 / 24.0))
VMEM_LIMIT = 50 * 1024 * 1024
AXES = ("tm", "gx", "gy")
ANY = pl.BlockSpec(memory_space=pl.ANY)
VM = pl.BlockSpec(memory_space=pltpu.VMEM)
SM = pl.BlockSpec(memory_space=pltpu.SMEM)
f32 = jnp.float32


def params(**kw):
    return pltpu.CompilerParams(vmem_limit_bytes=VMEM_LIMIT, **kw)


def shape(*dims):
    return jax.ShapeDtypeStruct(dims, f32)


def partner(i, color, size):
    j = i + 1 if (i + color) % 2 == 0 else i - 1
    return j if 0 <= j < size else None


def colors(size):
    return [k for k in (0, 1) if any(partner(i, k, size) is not None for i in range(size))]


def routes(sizes, cx, cy, hop):
    nt, nx, ny = sizes
    out = []
    for t in range(nt):
        if hop is not None and t != hop:
            continue
        for x in range(nx):
            px = x if cx is None else partner(x, cx, nx)
            for y in range(ny):
                py = y if cy is None else partner(y, cy, ny)
                if px is None or py is None:
                    continue
                target = t if hop is None else t + 1
                out.append(((t * nx + px) * ny + py, (target * nx + x) * ny + y))
    return out


def message_keys(nx, ny):
    keys = [(k, None) for k in colors(nx)]
    keys += [(k, l) for k in colors(nx) for l in colors(ny)]
    keys += [(None, l) for l in colors(ny)]
    return keys


def upper(axis, color):
    return lax.rem(lax.axis_index(axis) + color, 2) == 0


def pick(cond, a, b):
    return jnp.where(cond, jnp.int32(a), jnp.int32(b))


def times(steps, sect):
    h = steps[sect].astype(f32) * STEP_UNIT
    return h, 0.5 * h


def reaction(v):
    return v - v * v * v


def run_copies(pairs, sems):
    copies = [pltpu.make_async_copy(a, b, sems.at[i]) for i, (a, b) in enumerate(pairs)]
    for c in copies:
        c.start()
    for c in copies:
        c.wait()


def pack_kernel(keys, u, *rest):
    outs, sems = rest[:-1], rest[-1]
    nx, ny = u.shape[1], u.shape[2]
    pairs = []
    for (k, l), o in zip(keys, outs):
        xs = pl.ds(0, nx) if k is None else pl.ds(pick(upper("gx", k), nx - FW, 0), FW)
        ys = pl.ds(0, ny) if l is None else pl.ds(pl.multiple_of(pick(upper("gy", l), ny - YW, 0), 8), YW)
        pairs.append((u.at[:, xs, ys, :], o))
    run_copies(pairs, sems)


def coefficient_kernel(local, whole_tiles, kinds, diffs, steps, fine, coarse):
    tx, ty = local
    wx, wy = whole_tiles
    _, a = times(steps, lax.axis_index("tm"))
    x0 = lax.axis_index("gx") * tx
    y0 = lax.axis_index("gy") * ty
    sub = lax.broadcasted_iota(jnp.int32, (8, 128), 0)

    def value(i, j):
        ok = (i >= 0) & (i < wx) & (j >= 0) & (j < wy)
        kind = kinds[jnp.clip(i, 0, wx - 1), jnp.clip(j, 0, wy - 1)]
        return jnp.where(ok, diffs[kind], 0.0)

    ft = FW // TILE

    def fine_row(i, _):
        for jt in range(fine.shape[2] // 8):
            base = y0 - YW // TILE + jt * 2
            k = jnp.where(sub < 4, value(x0 - ft + i, base), value(x0 - ft + i, base + 1))
            inv = 1.0 / (1.0 + a * k * 6.0)
            at = pl.ds(jt * 8, 8)
            fine[0, i, at, :] = k
            fine[1, i, at, :] = a * k * inv
            fine[2, i, at, :] = inv
        return 0

    lax.fori_loop(0, fine.shape[1], fine_row, 0)
    ct = CW // 2

    def coarse_row(i, _):
        for jt in range(coarse.shape[2] // 8):
            base = y0 - YW // 2 + jt * 4
            v = [value(x0 - ct + i, base + q) for q in range(4)]
            k = jnp.where(sub < 4, jnp.where(sub < 2, v[0], v[1]), jnp.where(sub < 6, v[2], v[3]))
            inv = 1.0 / (1.0 + a * k * 3.0)
            at = pl.ds(jt * 8, 8)
            coarse[0, i, at, :] = a * k * inv
            coarse[1, i, at, :] = inv
        return 0

    lax.fori_loop(0, coarse.shape[1], coarse_row, 0)


def neighbours(ref, x, masks):
    c = ref[x]
    rows = c.shape[0]
    px = ref[x + 1] + ref[x - 1]
    py = pltpu.roll(c, 1, 0) + pltpu.roll(c, rows - 1, 0)
    z = pltpu.roll(c, 1, 1) * masks[0] + pltpu.roll(c, 127, 1) * masks[1]
    return c, px + py, z


def z_masks(rows):
    lane = lax.broadcasted_iota(jnp.int32, (rows, 128), 1)
    return (jnp.where(lane == 0, 0.0, 1.0), jnp.where(lane == 127, 0.0, 1.0))


def fine_kernel(keys, ckeys, steps, u, fine, *rest):
    nmsg = len(keys)
    msgs, rest = rest[:nmsg], rest[nmsg:]
    w1o, w2o, co = rest[:3]
    nc = len(ckeys)
    couts, rest = rest[3 : 3 + nc], rest[3 + nc :]
    ue, f0, q0, qa, qb, p2, w1, w2, tmp, sems = rest
    nx, ny = u.shape[1], u.shape[2]
    ye = ny + 2 * YW
    h, a = times(steps, lax.axis_index("tm"))
    gx, ngx = lax.axis_index("gx"), lax.axis_size("gx")
    low, high = gx > 0, gx < ngx - 1
    zero = jnp.zeros((ye, 128), f32)
    bufs = [q0, qa, qb, w1, w2]

    @pl.when(jnp.logical_not(low))
    def _():
        for j in range(3):
            ue[j, FW - 1] = zero
        for b in bufs:
            b[FW - 1] = zero

    @pl.when(jnp.logical_not(high))
    def _():
        for j in range(3):
            ue[j, FW + nx] = zero
        for b in bufs:
            b[FW + nx] = zero

    if len(colors(lax.axis_size("gy"))) < 2:
        def clear(i, _):
            for j in range(3):
                ue[j, i] = zero
            return 0
        lax.fori_loop(0, ue.shape[1], clear, 0)

    pairs = [(u, ue.at[:, pl.ds(FW, nx), pl.ds(YW, ny), :])]
    for (k, l), m in zip(keys, msgs):
        xs = pl.ds(FW, nx) if k is None else pl.ds(pick(upper("gx", k), FW + nx, 0), FW)
        ys = pl.ds(YW, ny) if l is None else pl.ds(pl.multiple_of(pick(upper("gy", l), YW + ny, 0), 8), YW)
        pairs.append((m, ue.at[:, xs, ys, :]))
    run_copies(pairs, sems)
    masks = z_masks(ye)

    def rows(r, body):
        first = FW - jnp.where(low, r, 0)
        last = FW + nx + jnp.where(high, r, 0)
        lax.fori_loop(first, last, lambda x, _: (body(x), 0)[1], 0)

    def kap(n, x):
        return fine[n, lax.div(x, TILE)]

    def stage1(x):
        k = kap(0, x)
        c, f = [], []
        for j in range(3):
            cj, pj, zj = neighbours(ue.at[j], x, masks)
            c.append(cj)
            f.append(reaction(cj) + k * (pj + zj - 6.0 * cj))
        f0[x] = f[0]
        h0 = WEIGHTS[0][0] * f[0] + WEIGHTS[0][1] * f[1] + WEIGHTS[0][2] * f[2]
        h1 = WEIGHTS[1][0] * f[0] + WEIGHTS[1][1] * f[1] + WEIGHTS[1][2] * f[2]
        q0[x] = (c[0] + h * h0 - c[1]) * kap(2, x)
        p2[x] = h * h1 - c[2] - a * reaction(c[1])

    rows(7, stage1)

    def jacobi(src, start, x):
        _, p, z = neighbours(src, x, masks)
        return start[x] + kap(1, x) * (p + z)

    def into(dst, src, start):
        def body(x):
            dst[x] = jacobi(src, start, x)
        return body

    rows(6, into(qa, q0, q0))
    rows(5, into(qb, qa, q0))

    def end1(x):
        w = ue[1, x] + jacobi(qb, q0, x)
        w1[x] = w
        p2[x] = (w + a * reaction(w) + p2[x]) * kap(2, x)

    rows(4, end1)

    @pl.when(jnp.logical_not(low))
    def _():
        p2[FW - 1] = zero

    @pl.when(jnp.logical_not(high))
    def _():
        p2[FW + nx] = zero

    rows(3, into(qa, p2, p2))
    rows(2, into(qb, qa, p2))

    def end2(x):
        w2[x] = ue[2, x] + jacobi(qb, p2, x)

    rows(1, end2)

    def halve(slot, v):
        tmp[slot] = v
        n = ny // 2
        return tmp[slot, pl.ds(YW, n, stride=2), :] + tmp[slot, pl.ds(YW + 1, n, stride=2), :]

    def coarse_row(i, _):
        sums = [0.0] * 5
        for d in range(2):
            x = FW + 2 * i + d
            k = kap(0, x)
            u0 = ue[0, x]
            g = [f0[x]]
            w = [u0]
            for ref in (w1, w2):
                c, p, z = neighbours(ref, x, masks)
                w.append(c)
                g.append(reaction(c) + k * (p + z - 6.0 * c))
            for m, ref in ((1, w1o), (2, w2o)):
                ref[2 * i + d] = w[m][YW : YW + ny]
            for m in range(2):
                sums[m] = sums[m] + (WEIGHTS[m][0] * g[0] + WEIGHTS[m][1] * g[1] + WEIGHTS[m][2] * g[2])
            for m in range(3):
                sums[2 + m] = sums[2 + m] + w[m]
        c0, c1, u0, u1, u2 = [halve(s, v) * 0.25 for s, v in enumerate(sums)]
        co[0, i] = h * c0 - a * reaction(u0) - u1
        co[1, i] = u1
        co[2, i] = h * c1 - a * reaction(u1) - u2
        co[3, i] = u0
        co[4, i] = u2
        return 0

    lax.fori_loop(0, nx // 2, coarse_row, 0)
    cx, cy = nx // 2, ny // 2
    fields = ((0, CW), (1, CN), (2, CN), (3, CW))
    for (k, l), o in zip(ckeys, couts):
        ys = pl.ds(0, cy) if l is None else pl.ds(pl.multiple_of(pick(upper("gy", l), cy - YW, 0), 8), YW)
        at = 0
        for fld, width in fields:
            if k is None:
                width, first = cx, 0
            else:
                first = pick(upper("gx", k), cx - width, 0)
            o[pl.ds(at, width)] = co[fld, pl.ds(first, width), ys, :]
            at += width


def assemble_kernel(keys, co, *rest):
    nm = len(keys)
    msgs, (ge, ce), sems = rest[:nm], rest[nm : nm + 2], rest[nm + 2]
    cx, cy = co.shape[1], co.shape[2]
    zero = jnp.zeros(ge.shape[1:], f32)
    for f in range(3):
        ge[f] = zero
    ce[...] = zero
    fields = ((0, CW), (1, CN), (2, CN), (3, CW))
    pairs = []

    def target(f):
        return ce if f == 3 else ge.at[f]

    for f, _ in fields:
        pairs.append((co.at[f], target(f).at[pl.ds(CW, cx), pl.ds(YW, cy), :]))
    for (k, l), m in zip(keys, msgs):
        ys = pl.ds(YW, cy) if l is None else pl.ds(pl.multiple_of(pick(upper("gy", l), YW + cy, 0), 8), YW)
        at = 0
        for f, width in fields:
            if k is None:
                width, first = cx, CW
            else:
                first = pick(upper("gx", k), CW + cx, CW - width)
            pairs.append((m.at[pl.ds(at, width)], target(f).at[pl.ds(first, width), ys, :]))
            at += width
    run_copies(pairs, sems)


def chain_kernel(turn, keys, steps, ge, coef, co, *rest):
    first = turn == 0
    if first:
        ce, rest = rest[0], rest[1:]
        nm = 0
    else:
        old, own, rest = rest[0], rest[1], rest[2:]
        nm = len(keys)
        msgs, rest = rest[:nm], rest[nm:]
    state = rest[0]
    rest = rest[1:]
    no = len(keys)
    couts, rest = rest[:no], rest[no:]
    cin, q0, qa, qb, sems = rest
    cx, cy = co.shape[1], co.shape[2]
    ye = cy + 2 * YW
    sect = lax.axis_index("tm")
    h, a = times(steps, sect)
    gx, ngx = lax.axis_index("gx"), lax.axis_size("gx")
    low, high = gx > 0, gx < ngx - 1

    @pl.when(sect == turn)
    def _():
        zero = jnp.zeros((ye, 128), f32)
        for b in (q0, qa, qb):
            b[CW - 1] = zero
            b[CW + cx] = zero
        if first:
            c = ce
        else:
            c = cin
            if len(colors(ngx)) < 2 or len(colors(lax.axis_size("gy"))) < 2:
                cin[...] = jnp.zeros(cin.shape, f32)
            pairs = [(own, cin.at[pl.ds(CW, cx), pl.ds(YW, cy), :])]
            for (k, l), m in zip(keys, msgs):
                xs = pl.ds(CW, cx) if k is None else pl.ds(pick(upper("gx", k), CW + cx, 0), CW)
                ys = pl.ds(YW, cy) if l is None else pl.ds(pl.multiple_of(pick(upper("gy", l), YW + cy, 0), 8), YW)
                pairs.append((m, cin.at[xs, ys, :]))
            run_copies(pairs, sems)
        masks = z_masks(ye)

        def rows(r, body):
            begin = CW - jnp.where(low, r, 0)
            end = CW + cx + jnp.where(high, r, 0)
            lax.fori_loop(begin, end, lambda x, _: (body(x), 0)[1], 0)

        def jacobi(src, x):
            _, p, z = neighbours(src, x, masks)
            return q0[x] + coef[0, lax.div(x, 2)] * (0.25 * p + z)

        def into(dst, src):
            def body(x):
                dst[x] = jacobi(src, x)
            return body

        def start(x):
            v = c[x]
            q0[x] = (v + a * reaction(v) + ge[0, x]) * coef[1, lax.div(x, 2)]

        rows(6, start)
        rows(5, into(qa, q0))
        rows(4, into(qb, qa))

        def middle(x):
            w = ge[1, x] + jacobi(qb, x)
            qa[x] = w

        rows(3, middle)

        def keep(i, _):
            state[0, i] = c[CW + i, YW : YW + cy]
            state[1, i] = qa[CW + i, YW : YW + cy]
            return 0

        lax.fori_loop(0, cx, keep, 0)

        def second(x):
            w = qa[x]
            q0[x] = (w + a * reaction(w) + ge[2, x]) * coef[1, lax.div(x, 2)]

        rows(3, second)

        @pl.when(jnp.logical_not(low))
        def _():
            qa[CW - 1] = zero

        @pl.when(jnp.logical_not(high))
        def _():
            qa[CW + cx] = zero

        rows(2, into(qa, q0))
        rows(1, into(qb, qa))

        def end(x):
            i = x - CW
            state[2, i] = co[4, i] + jacobi(qb, x)[YW : YW + cy]

        rows(0, end)
        for (k, l), o in zip(keys, couts):
            xs = pl.ds(0, cx) if k is None else pl.ds(pick(upper("gx", k), cx - CW, 0), CW)
            ys = pl.ds(0, cy) if l is None else pl.ds(pl.multiple_of(pick(upper("gy", l), cy - YW, 0), 8), YW)
            o[...] = state[2, xs, ys, :]


def finish_kernel(u0, arrived, w1, w2, state, co, out, tmp):
    sect = lax.axis_index("tm")
    ny = u0.shape[1]
    half = ny // 2

    def spread(slot, v):
        tmp[slot, pl.ds(0, half, stride=2), :] = v
        tmp[slot, pl.ds(1, half, stride=2), :] = v
        return tmp[slot]

    def row(i, _):
        base = [jnp.where(sect == 0, u0[2 * i + d], arrived[2 * i + d]) for d in range(2)]
        tmp[3] = base[0] + base[1]
        low = (tmp[3, pl.ds(0, half, stride=2), :] + tmp[3, pl.ds(1, half, stride=2), :]) * 0.25
        d0 = spread(0, state[0, i] - low)
        d1 = spread(1, state[1, i] - co[1, i])
        d2 = spread(2, state[2, i] - co[4, i])
        for d in range(2):
            out[0, 2 * i + d] = base[d] + d0
            out[1, 2 * i + d] = w1[2 * i + d] + d1
            out[2, 2 * i + d] = w2[2 * i + d] + d2
        return 0

    lax.fori_loop(0, u0.shape[0] // 2, row, 0)


def per_device(sizes, fine_nodes, section_steps, diffusivities, tile_kinds):
    nt, ngx, ngy = sizes
    u = fine_nodes[0]
    nodes, nx, ny, cz = u.shape
    cx, cy = nx // 2, ny // 2
    keys = message_keys(ngx, ngy)
    nk = len(keys)

    def dims(k, l, wx, lx, ly):
        return (lx if k is None else wx, ly if l is None else YW, cz)

    def send(arrays, hop):
        return [lax.ppermute(v, AXES, routes(sizes, k, l, hop)) for (k, l), v in zip(keys, arrays)]

    packed = pl.pallas_call(
        functools.partial(pack_kernel, keys),
        out_shape=[shape(nodes, *dims(k, l, FW, nx, ny)) for k, l in keys],
        in_specs=[ANY],
        out_specs=[ANY] * nk,
        scratch_shapes=[pltpu.SemaphoreType.DMA((nk,))],
        compiler_params=params(),
        name="pack",
    )(u)
    halos = send(packed, None)

    kinds = lax.all_gather(tile_kinds, "gy", axis=1, tiled=True)
    kinds = lax.all_gather(kinds, "gx", axis=0, tiled=True)
    fye, cye = ny + 2 * YW, cy + 2 * YW
    fine, coef = pl.pallas_call(
        functools.partial(coefficient_kernel, tile_kinds.shape, kinds.shape),
        out_shape=[shape(3, (nx + 2 * FW) // TILE, fye, cz), shape(2, (cx + 2 * CW) // 2, cye, cz)],
        in_specs=[SM, SM, SM],
        out_specs=[VM, VM],
        compiler_params=params(),
        name="coefficients",
    )(kinds, diffusivities, section_steps)

    xe = nx + 2 * FW
    buf = pltpu.VMEM((xe, fye, cz), f32)
    depth = 2 * CW + 2 * CN
    out = pl.pallas_call(
        functools.partial(fine_kernel, keys, keys),
        out_shape=[shape(nx, ny, cz), shape(nx, ny, cz), shape(5, cx, cy, cz)]
        + [shape(*dims(k, l, depth, 4 * cx, cy)) for k, l in keys],
        in_specs=[SM, ANY, VM] + [ANY] * nk,
        out_specs=[VM] * (3 + nk),
        scratch_shapes=[pltpu.VMEM((3, xe, fye, cz), f32)] + [buf] * 7
        + [pltpu.VMEM((5, fye, cz), f32), pltpu.SemaphoreType.DMA((nk + 1,))],
        compiler_params=params(),
        name="fine_sweep",
    )(section_steps, u, fine, *halos)
    w1, w2, co = out[:3]
    strips = send(out[3:], None)
    arrived = lax.ppermute(w2, "tm", [(i, i + 1) for i in range(nt - 1)])

    ncopy = 4 + 4 * nk
    ge, ce = pl.pallas_call(
        functools.partial(assemble_kernel, keys),
        out_shape=[shape(3, cx + 2 * CW, cye, cz), shape(cx + 2 * CW, cye, cz)],
        in_specs=[ANY] + [ANY] * nk,
        out_specs=[VM, VM],
        scratch_shapes=[pltpu.SemaphoreType.DMA((ncopy,))],
        compiler_params=params(),
        name="assemble",
    )(co, *strips)

    state, handed = None, None
    cbuf = pltpu.VMEM((cx + 2 * CW, cye, cz), f32)
    for n in range(nt):
        last = n == nt - 1
        args = [section_steps, ge, coef, co]
        specs = [SM, VM, VM, VM]
        alias = {}
        if n == 0:
            args.append(ce)
            specs.append(VM)
        else:
            alias = {len(args): 0}
            args += [state] + handed
            specs += [VM] + [ANY] * len(handed)
        res = pl.pallas_call(
            functools.partial(chain_kernel, n, keys),
            out_shape=[shape(3, cx, cy, cz)] + [shape(*dims(k, l, CW, cx, cy)) for k, l in keys],
            in_specs=specs,
            out_specs=[VM] * (1 + nk),
            scratch_shapes=[cbuf] * 4 + [pltpu.SemaphoreType.DMA((nk + 1,))],
            input_output_aliases=alias,
            compiler_params=params(),
            name=f"chain_{n}",
        )(*args)
        state = res[0]
        if not last:
            own = lax.ppermute(state[2], AXES, routes(sizes, None, None, n))
            handed = [own] + send(res[1:], n)

    blk = 8
    fspec = pl.BlockSpec((blk, ny, cz), lambda i: (i, 0, 0))
    result = pl.pallas_call(
        finish_kernel,
        grid=(nx // blk,),
        out_shape=shape(3, nx, ny, cz),
        in_specs=[fspec] * 4
        + [pl.BlockSpec((3, blk // 2, cy, cz), lambda i: (0, i, 0, 0)), pl.BlockSpec((5, blk // 2, cy, cz), lambda i: (0, i, 0, 0))],
        out_specs=pl.BlockSpec((3, blk, ny, cz), lambda i: (0, i, 0, 0)),
        scratch_shapes=[pltpu.VMEM((4, ny, cz), f32)],
        compiler_params=params(),
        name="finish",
    )(u[0], arrived, w1, w2, state, co)
    return result[None]


def solution(mesh):
    sizes = tuple(mesh.shape[a] for a in AXES)
    return jax.shard_map(
        functools.partial(per_device, sizes),
        mesh=mesh,
        in_specs=(P("tm", None, "gx", "gy", None), P(), P(), P("gx", "gy")),
        out_specs=P("tm", None, "gx", "gy", None),
        check_vma=False,
    )
```

```python
import functools
import jax
import jax.numpy as jnp
from jax import lax
from jax.experimental import pallas as pl
from jax.experimental.pallas import tpu as pltpu
from jax.sharding import PartitionSpec as P

TILE = 4
FW = 8
CW = 6
CN = 3
FEW, MANY = 2, 4
YW = 8
STEP_UNIT = 0.05
WEIGHTS = ((5.0 / 24.0, 1.0 / 3.0, -1.0 / 24.0), (-1.0 / 24.0, 1.0 / 3.0, 5.0 / 24.0))
AXES = ("tm", "gx", "gy")
ANY = pl.BlockSpec(memory_space=pl.ANY)
VM = pl.BlockSpec(memory_space=pltpu.VMEM)
SM = pl.BlockSpec(memory_space=pltpu.SMEM)
f32 = jnp.float32


def params(mib):
    return pltpu.CompilerParams(vmem_limit_bytes=mib * 1024 * 1024)


def shape(*dims):
    return jax.ShapeDtypeStruct(dims, f32)


def partner(i, color, size):
    j = i + 1 if (i + color) % 2 == 0 else i - 1
    return j if 0 <= j < size else None


def colors(size):
    return [k for k in (0, 1) if any(partner(i, k, size) is not None for i in range(size))]


def routes(sizes, cx, cy, hop):
    nt, nx, ny = sizes
    out = []
    for t in range(nt):
        if hop is not None and t != hop:
            continue
        for x in range(nx):
            px = x if cx is None else partner(x, cx, nx)
            for y in range(ny):
                py = y if cy is None else partner(y, cy, ny)
                if px is None or py is None:
                    continue
                target = t if hop is None else t + 1
                out.append(((t * nx + px) * ny + py, (target * nx + x) * ny + y))
    return out


def message_keys(nx, ny):
    keys = [(k, None) for k in colors(nx)]
    keys += [(k, l) for k in colors(nx) for l in colors(ny)]
    keys += [(None, l) for l in colors(ny)]
    return keys


def upper(axis, color):
    return lax.rem(lax.axis_index(axis) + color, 2) == 0


def pick(cond, a, b):
    return jnp.where(cond, jnp.int32(a), jnp.int32(b))


def times(steps, sect):
    h = steps[sect].astype(f32) * STEP_UNIT
    return h, 0.5 * h


def reaction(v):
    return v - v * v * v


def run_copies(pairs, sems):
    copies = [pltpu.make_async_copy(a, b, sems.at[i]) for i, (a, b) in enumerate(pairs)]
    for c in copies:
        c.start()
    for c in copies:
        c.wait()


def table_rows(rows, tiles):
    return -(-tiles // rows)


def table_copies(table, msg, base, out):
    tiles, height = table.shape[0], msg.shape[1]
    pairs = []
    for i in range(table_rows(height, tiles)):
        n = min(height, tiles - i * height)
        pair = (table.at[pl.ds(i * height, n)], msg.at[base + i, pl.ds(0, n)])
        pairs.append(pair if out else pair[::-1])
    return pairs


def pack_kernel(keys, u, table, *rest):
    outs, sems = rest[:-1], rest[-1]
    nx, ny = u.shape[1], u.shape[2]
    pairs = []
    for (k, l), o in zip(keys, outs):
        w = nx if k is None else FW
        xs = pl.ds(0 if k is None else pick(upper("gx", k), nx - FW, 0), w)
        ys = pl.ds(0, ny) if l is None else pl.ds(pl.multiple_of(pick(upper("gy", l), ny - YW, 0), 8), YW)
        pairs += [(u.at[j, xs, ys, :], o.at[pl.ds(j * w, w)]) for j in range(3)]
        pairs += table_copies(table, o, 3 * w, True)
    run_copies(pairs, sems)


def permuted(ref, *lead):
    t_count = ref.shape[-2] // 8
    return jnp.concatenate([ref[(*lead, pl.ds(t, 8, stride=t_count))] for t in range(t_count)], axis=-2)


def store_plain(ref, lead, value):
    t_count = value.shape[-2] // 8
    for t in range(t_count):
        ref[(*lead, pl.ds(t, 8, stride=t_count))] = value[..., t * 8 : t * 8 + 8, :]


def expand(tables, tx, ty, row, piece, cells):
    sub = lax.broadcasted_iota(jnp.int32, (8, 128), 0)
    lane = lax.broadcasted_iota(jnp.int32, (8, 128), 1)
    if isinstance(row, int):
        sx = 0 if row < 0 else (2 if row >= tx else 1)
        r = row - (sx - 1) * tx
    else:
        sx = jnp.where(row < 0, 0, jnp.where(row >= tx, 2, 1))
        r = row - (sx - 1) * tx
    runs = ty * cells // 8
    per = 8 // cells
    sy, first = (0, ty - per) if piece < 0 else ((2, 0) if piece >= runs else (1, piece * per))
    hot = lane == first + lax.div(sub, cells)
    return jnp.sum(jnp.where(hot, tables[sx, sy, pl.ds(r, 1), :], 0.0), axis=1, keepdims=True)


def fill_coefficients(tables, local, cells, low, rows, plain, write):
    tx, ty = local
    count = plain.shape[1] // 8
    for i in range(rows):
        slot = i % plain.shape[0]
        for p in range(count):
            k = expand(tables, tx, ty, low + i, p - 1, cells)
            plain[slot, p * 8 : p * 8 + 8, :] = jnp.broadcast_to(k, (8, 128))
        write(i, jnp.concatenate([plain[slot, pl.ds(t, 8, stride=count), :] for t in range(count)], axis=0))


def coarse_coefficient_kernel(local, steps, tables, coarse, plain):
    _, a = times(steps, lax.axis_index("tm"))

    def write(i, k):
        inv = 1.0 / (1.0 + a * k * 3.0)
        coarse[0, i] = a * k * inv
        coarse[1, i] = inv

    rows = local[0] + CW
    fill_coefficients(tables, local, TILE // 2, -(CW // 2), rows, plain, write)
    for i in range(rows, coarse.shape[1]):
        write(i, jnp.zeros(plain.shape[1:], f32))


def neighbours(v, masks):
    c = v[1:-1]
    px = v[2:] + v[:-2]
    before = jnp.concatenate([pltpu.roll(c[:, -8:], 1, 1), c[:, :-8]], axis=1)
    after = jnp.concatenate([c[:, 8:], pltpu.roll(c[:, :8], 7, 1)], axis=1)
    z = pltpu.roll(c, 1, 2) * masks[0] + pltpu.roll(c, 127, 2) * masks[1]
    return c, px + (before + after), z


def z_masks():
    lane = lax.broadcasted_iota(jnp.int32, (1, 8, 128), 2)
    return (jnp.where(lane == 0, 0.0, 1.0), jnp.where(lane == 127, 0.0, 1.0))


def wide_masks(rows, y):
    return tuple(jnp.concatenate([jnp.concatenate([m] * (y // 8), axis=1)] * rows, axis=0) for m in z_masks())


def sweep_rows(own, width, r, step, body):
    gx, ngx = lax.axis_index("gx"), lax.axis_size("gx")
    n = own + r * min(ngx - 1, 2)
    pad = -n % step
    if ngx == 2:
        begin = width - pick(gx > 0, r, pad)
    else:
        begin = width - r * min(ngx - 1, 2) // 2
    lax.fori_loop(0, (n + pad) // step, lambda i, _: (body(begin + i * step), 0)[1], 0)


def clear_walls(width, own, bufs, count=4):
    gx, ngx = lax.axis_index("gx"), lax.axis_size("gx")
    for b in bufs:
        zero = jnp.zeros((count,) + b.shape[1:], f32)

        @pl.when(gx == 0)
        def _():
            b[width - count : width] = zero

        @pl.when(gx == ngx - 1)
        def _():
            b[width + own : width + own + count] = zero


SEAM = 12
FIELDS = 10


class Stages:
    def __init__(self, u, f0, q0, qa, qb, p2, w1, w2, fine, h, a, tile_of):
        self.u, self.f0, self.q0, self.qa, self.qb, self.p2, self.w1, self.w2 = u, f0, q0, qa, qb, p2, w1, w2
        self.fine, self.h, self.a, self.tile_of = fine, h, a, tile_of

    def coef(self, n, x, step):
        return jnp.stack([self.fine[n, self.tile_of(x + i)] for i in range(step)])

    def forces(self, x, step, masks):
        k, h, a = self.coef(0, x, step), self.h, self.a
        c, f = [], []
        for j in range(3):
            cj, pj, zj = neighbours(self.u(j, pl.ds(x - 1, step + 2)), masks)
            c.append(cj)
            f.append(reaction(cj) + k * (pj + zj - 6.0 * cj))
        at = pl.ds(x, step)
        self.f0[at] = f[0]
        h0 = WEIGHTS[0][0] * f[0] + WEIGHTS[0][1] * f[1] + WEIGHTS[0][2] * f[2]
        h1 = WEIGHTS[1][0] * f[0] + WEIGHTS[1][1] * f[1] + WEIGHTS[1][2] * f[2]
        self.q0[at] = (c[0] + h * h0 - c[1]) * self.coef(2, x, step)
        self.p2[at] = h * h1 - c[2] - a * reaction(c[1])

    def jacobi(self, src, start, x, step, masks):
        _, p, z = neighbours(src[pl.ds(x - 1, step + 2)], masks)
        return start[pl.ds(x, step)] + self.coef(1, x, step) * (p + z)

    def into(self, dst, src, start):
        def body(x, step, masks):
            dst[pl.ds(x, step)] = self.jacobi(src, start, x, step, masks)
        return body

    def end1(self, x, step, masks):
        at = pl.ds(x, step)
        w = self.u(1, at) + self.jacobi(self.qb, self.q0, x, step, masks)
        self.w1[at] = w
        self.p2[at] = (w + self.a * reaction(w) + self.p2[at]) * self.coef(2, x, step)

    def end2(self, x, step, masks):
        at = pl.ds(x, step)
        self.w2[at] = self.u(2, at) + self.jacobi(self.qb, self.p2, x, step, masks)

    def bodies(self):
        return [
            (1, self.forces),
            (2, self.into(self.qa, self.q0, self.q0)),
            (3, self.into(self.qb, self.qa, self.q0)),
            (4, self.end1),
            (5, self.into(self.qa, self.p2, self.p2)),
            (6, self.into(self.qb, self.qa, self.p2)),
            (7, self.end2),
        ]

    def coarse_pair(self, x, i, w1o, w2o, co, plain, tmp, ny):
        ye = ny + 2 * YW
        masks = wide_masks(2, ye)
        h, a = self.h, self.a

        def pair_sum(v):
            v = v[0] + v[1]
            return jnp.concatenate([v[t : t + 8] + v[t + 8 : t + 16] for t in range(0, ye, 16)], axis=0)

        at = pl.ds(x, 2)
        k = self.coef(0, x, 2)
        g = [self.f0[at]]
        w = [self.u(0, at)]
        for m, (ref, out) in enumerate(((self.w1, w1o), (self.w2, w2o))):
            c, p, z = neighbours(ref[pl.ds(x - 1, 4)], masks)
            w.append(c)
            g.append(reaction(c) + k * (p + z - 6.0 * c))
            store_plain(tmp, (2 * m + 0,), c[0])
            store_plain(tmp, (2 * m + 1,), c[1])
            out[pl.ds(2 * i, 2)] = tmp[2 * m : 2 * m + 2, YW : YW + ny]
        c0, c1 = [pair_sum(wt[0] * g[0] + wt[1] * g[1] + wt[2] * g[2]) * 0.25 for wt in WEIGHTS]
        u0, u1, u2 = [pair_sum(v) * 0.25 for v in w]
        values = (h * c0 - a * reaction(u0) - u1, u1, h * c1 - a * reaction(u1) - u2, u0, u2)
        for n, v in enumerate(values):
            store_plain(plain, (n,), v)
            co[n, i] = plain[n, YW // 2 : YW // 2 + ny // 2]


def seam_count(size):
    return min(size - 1, 2)


def seam_is_low(seam):
    return lax.axis_index("gx") > 0 if lax.axis_size("gx") == 2 else seam == 0


def target_y(l, ny):
    return pl.ds(YW, ny) if l is None else pl.ds(pl.multiple_of(pick(upper("gy", l), YW + ny, 0), 8), YW)


def inner_kernel(keys, local, seams, steps, u, table, *rest):
    nmsg = len(keys)
    msgs, rest = rest[:nmsg], rest[nmsg:]
    w1o, w2o, co, seam, rest = rest[0], rest[1], rest[2], rest[3], rest[4:]
    ue, f0, q0, qa, qb, p2, w1, w2, fine, tables, plain, tmp, sems = rest
    nx, ny = u.shape[1], u.shape[2]
    ye = ny + 2 * YW
    h, a = times(steps, lax.axis_index("tm"))

    if nmsg < 2:
        def clear(i, _):
            for j in range(3):
                ue[j, i] = jnp.zeros((ye, 128), f32)
            return 0
        lax.fori_loop(0, ue.shape[1], clear, 0)
    clear_walls(FW, nx, [ue.at[0], ue.at[1], ue.at[2], q0, qa, qb, p2, w1, w2])
    for j in (0, 2):
        tables[1, j] = jnp.zeros(tables.shape[2:], f32)
    pairs = [(u, ue.at[:, pl.ds(FW, nx), pl.ds(YW, ny), :])]
    for (_, l), m in zip(keys, msgs):
        pairs += [(m.at[pl.ds(j * nx, nx)], ue.at[j, pl.ds(FW, nx), target_y(l, ny), :]) for j in range(3)]
        pairs += table_copies(tables.at[1, pick(upper("gy", l), 2, 0)], m, 3 * nx, False)
    pairs.append((table, tables.at[1, 1]))
    run_copies(pairs, sems)

    def write(i, k):
        inv = 1.0 / (1.0 + a * k * 6.0)
        fine[0, i] = k
        fine[1, i] = a * k * inv
        fine[2, i] = inv

    ft = FW // TILE
    for i in list(range(ft)) + list(range(ft + local[0], fine.shape[1])):
        write(i, jnp.zeros((ye, 128), f32))
    fill_coefficients(tables, local, TILE, 0, local[0], tmp, lambda i, k: write(ft + i, k))
    st = Stages(
        lambda j, at: permuted(ue, j, at), f0, q0, qa, qb, p2, w1, w2, fine, h, a, lambda x: lax.div(x, TILE)
    )
    for k, body in st.bodies():
        step = FEW if k == 1 else MANY
        if seams == 2 and (nx - 2 * k) % step:
            step = 2
        masks = wide_masks(step, ye)
        sweep_rows(nx, FW, -k, step, functools.partial(lambda body, step, masks, x: body(x, step, masks), body, step, masks))

    def coarse_rows(x):
        st.coarse_pair(x, lax.div(x - FW, 2), w1o, w2o, co, plain, tmp, ny)

    sweep_rows(nx, FW, -8, 2, coarse_rows)
    for n in range(seams):
        low = seam_is_low(n)
        src, dst = pick(low, FW, FW + nx - SEAM), pick(low, FW, 0)

        def keep(i, _):
            x, to = pl.ds(src + 4 * i, 4), pl.ds(dst + 4 * i, 4)
            for j in range(3):
                seam[n, j, to] = permuted(ue, j, x)
            for j, b in enumerate((f0, q0, qa, qb, p2, w1, w2)):
                seam[n, 3 + j, to] = b[x]
            return 0

        lax.fori_loop(0, SEAM // 4, keep, 0)


def seam_kernel(keys, ckeys, local, seams, steps, table, *rest):
    nmsg = len(keys)
    msgs, rest = rest[:nmsg], rest[nmsg + 4 :]
    w1o, w2o, co, seam, tables = rest[:5]
    nc = len(ckeys)
    couts, rest = rest[5 : 5 + nc], rest[5 + nc :]
    halo, fine, plain, tmp, sems = rest
    nx, ny = w1o.shape[0], w1o.shape[1]
    ye = ny + 2 * YW
    h, a = times(steps, lax.axis_index("tm"))
    for i in range(3):
        for j in range(3):
            if (i, j) != (1, 1):
                tables[i, j] = jnp.zeros(tables.shape[2:], f32)
    if len(colors(lax.axis_size("gy"))) < 2 or len(colors(lax.axis_size("gx"))) < min(seams, 2):
        halo[...] = jnp.zeros(halo.shape, f32)
    pairs = []
    for (k, l), m in zip(keys, msgs):
        w = nx if k is None else FW
        if k is not None:
            n = 0 if seams == 1 else pick(upper("gx", k), 1, 0)
            pairs += [(m.at[pl.ds(j * w, w)], halo.at[n, j, :, target_y(l, ny), :]) for j in range(3)]
        sx = 1 if k is None else pick(upper("gx", k), 2, 0)
        sy = 1 if l is None else pick(upper("gy", l), 2, 0)
        pairs += table_copies(tables.at[sx, sy], m, 3 * w, False)
    pairs.append((table, tables.at[1, 1]))
    run_copies(pairs, sems)
    tx = local[0]
    for n in range(seams):
        low = seam_is_low(n)

        def write(i, k):
            inv = 1.0 / (1.0 + a * k * 6.0)
            fine[0, i] = k
            fine[1, i] = a * k * inv
            fine[2, i] = inv

        fill_coefficients(
            tables, local, TILE, pick(low, -(FW // TILE), tx - SEAM // TILE), fine.shape[1], tmp, write
        )
        to = pick(low, 0, SEAM)
        for i in range(0, FW, 4):
            for j in range(3):
                seam[n, j, pl.ds(to + i, 4)] = permuted(halo, n, j, pl.ds(i, 4))
        st = Stages(
            lambda j, at: seam[n, j, at], *[seam.at[n, 3 + j] for j in range(7)], fine, h, a, lambda x: lax.div(x, TILE)
        )
        for k, body in st.bodies():
            step = FEW if k == 1 else MANY
            masks = wide_masks(step, ye)
            first = pick(low, k, SEAM - k)
            lax.fori_loop(0, 8 // step, lambda i, _: (body(first + i * step, step, masks), 0)[1], 0)
        first = pick(low, FW, SEAM - 8)
        row = pick(low, 0, nx // 2 - 4)
        lax.fori_loop(
            0, 4, lambda i, _: (st.coarse_pair(first + 2 * i, row + i, w1o, w2o, co, plain, tmp, ny), 0)[1], 0
        )
    cx, cy = nx // 2, ny // 2
    fields = ((0, CW), (1, CN), (2, CN), (3, CW))
    for (k, l), o in zip(ckeys, couts):
        ys = pl.ds(0, cy) if l is None else pl.ds(pl.multiple_of(pick(upper("gy", l), cy - YW, 0), 8), YW)
        at = 0
        for fld, width in fields:
            if k is None:
                width, first = cx, 0
            else:
                first = pick(upper("gx", k), cx - width, 0)
            o[pl.ds(at, width)] = co[fld, pl.ds(first, width), ys, :]
            at += width


def assemble_kernel(keys, co, *rest):
    nm = len(keys)
    msgs, (gp, ce, ge), sems = rest[:nm], rest[nm : nm + 3], rest[nm + 3]
    cx, cy = co.shape[1], co.shape[2]

    def clear(i, _):
        for f in range(3):
            ge[f, i] = jnp.zeros(ge.shape[2:], f32)
        ce[i] = jnp.zeros(ge.shape[2:], f32)
        return 0

    lax.fori_loop(0, ce.shape[0], clear, 0)
    fields = ((0, CW), (1, CN), (2, CN), (3, CW))
    pairs = []

    def target(f):
        return ce if f == 3 else ge.at[f]

    for f, _ in fields:
        pairs.append((co.at[f], target(f).at[pl.ds(CW, cx), pl.ds(YW, cy), :]))
    for (k, l), m in zip(keys, msgs):
        ys = pl.ds(YW, cy) if l is None else pl.ds(pl.multiple_of(pick(upper("gy", l), YW + cy, 0), 8), YW)
        at = 0
        for f, width in fields:
            if k is None:
                width, first = cx, CW
            else:
                first = pick(upper("gx", k), CW + cx, CW - width)
            pairs.append((m.at[pl.ds(at, width)], target(f).at[pl.ds(first, width), ys, :]))
            at += width
    run_copies(pairs, sems)

    def order(i, _):
        at = pl.ds(2 * i, 2)
        for f in range(3):
            gp[f, at] = permuted(ge, f, at)
        return 0

    lax.fori_loop(0, ce.shape[0] // 2, order, 0)


def chain_kernel(turn, keys, arrive, steps, ge, coef, co, *rest):
    first = turn == 0
    if first:
        ce, rest = rest[0], rest[1:]
    else:
        _, own, rest = rest[0], rest[1], rest[2:]
        nm = len(arrive)
        msgs, rest = rest[:nm], rest[nm:]
        if turn == 1:
            rest = rest[1:]
    state = rest[0]
    rest = rest[1:]
    no = len(keys)
    whole, couts, rest = rest[0], rest[1 : 1 + no], rest[1 + no :]
    cin, q0, qa, qb, plain, sems = rest
    cx, cy = co.shape[1], co.shape[2]
    ye = cy + 2 * YW
    sect = lax.axis_index("tm")
    h, a = times(steps, sect)
    ngx, ngy = lax.axis_size("gx"), lax.axis_size("gy")

    @pl.when(sect == turn)
    def _():
        clear_walls(CW, cx, (q0, qa, qb))
        if first:
            c = ce
        else:
            c = cin
            if len(colors(ngy)) < 2:
                cin[...] = jnp.zeros(cin.shape, f32)
            else:
                clear_walls(CW, cx, (cin,))
            pairs = [(own, cin.at[pl.ds(CW, cx), pl.ds(YW, cy), :])]
            for (k, l), m in zip(arrive, msgs):
                if k is None:
                    xs = pl.ds(CW, cx)
                else:
                    xs = pl.ds(pick(upper("gx", k), CW + cx, 0), CW)
                ys = pl.ds(YW, cy) if l is None else pl.ds(pl.multiple_of(pick(upper("gy", l), YW + cy, 0), 8), YW)
                pairs.append((m, cin.at[xs, ys, :]))
            run_copies(pairs, sems)
        step = 4
        masks = wide_masks(step, ye)

        def rows(r, body):
            sweep_rows(cx, CW, r, step, body)

        def coefs(n, x):
            return jnp.stack([coef[n, lax.div(x + i, 2)] for i in range(step)])

        def jacobi(src, x):
            _, p, z = neighbours(src[pl.ds(x - 1, step + 2)], masks)
            return q0[pl.ds(x, step)] + coefs(0, x) * (0.25 * p + z)

        def into(dst, src):
            def body(x):
                dst[pl.ds(x, step)] = jacobi(src, x)
            return body

        def start(x):
            at = pl.ds(x, step)
            v = permuted(c, at)
            q0[at] = (v + a * reaction(v) + ge[0, at]) * coefs(1, x)

        rows(6, start)
        rows(5, into(qa, q0))
        rows(4, into(qb, qa))

        def middle(x):
            at = pl.ds(x, step)
            w = ge[1, at] + jacobi(qb, x)
            q0[at] = (w + a * reaction(w) + ge[2, at]) * coefs(1, x)
            store_plain(plain, (0, at), w)

        rows(3, middle)
        rows(2, into(qa, q0))
        rows(1, into(qb, qa))

        def end(x):
            store_plain(plain, (1, pl.ds(x, step)), jacobi(qb, x))

        rows(0, end)

        def keep(i, _):
            x, at = pl.ds(CW + 4 * i, 4), pl.ds(4 * i, 4)
            state[0, at] = c[x, YW : YW + cy]
            state[1, at] = plain[0, x, YW : YW + cy]
            state[2, at] = co[4, at] + plain[1, x, YW : YW + cy]
            whole[at] = state[2, at]
            return 0

        lax.fori_loop(0, cx // 4, keep, 0)
        for (k, l), o in zip(keys, couts):
            xs = pl.ds(0, cx) if k is None else pl.ds(pick(upper("gx", k), cx - CW, 0), CW)
            ys = pl.ds(0, cy) if l is None else pl.ds(pl.multiple_of(pick(upper("gy", l), cy - YW, 0), 8), YW)
            o[...] = state[2, xs, ys, :]


def finish_kernel(u0, arrived, w1, w2, state, co, out):
    sect = lax.axis_index("tm")
    ny = u0.shape[1]
    ft, ct = ny // 8, ny // 16

    def row(i, _):
        at = pl.ds(2 * i, 2)

        def fine_tile(ref, t):
            return ref[at, pl.ds(t, 8, stride=ft), :]

        def coarse_tile(ref, n, t):
            return ref[n, i, pl.ds(t, 8, stride=ct), :]

        for t in range(ct):
            base = [jnp.where(sect == 0, fine_tile(u0, 2 * t + d), fine_tile(arrived, 2 * t + d)) for d in range(2)]
            both = base[0] + base[1]
            d0 = coarse_tile(state, 0, t) - (both[0] + both[1]) * 0.25
            d1 = coarse_tile(state, 1, t) - coarse_tile(co, 1, t)
            d2 = coarse_tile(state, 2, t) - coarse_tile(co, 4, t)
            for d in range(2):
                to = pl.ds(2 * t + d, 8, stride=ft)
                out[0, at, to, :] = base[d] + d0
                out[1, at, to, :] = fine_tile(w1, 2 * t + d) + d1
                out[2, at, to, :] = fine_tile(w2, 2 * t + d) + d2
        return 0

    lax.fori_loop(0, u0.shape[0] // 2, row, 0)


def per_device(sizes, fine_nodes, section_steps, diffusivities, tile_kinds):
    nt, ngx, ngy = sizes
    u = fine_nodes[0]
    nodes, nx, ny, cz = u.shape
    cx, cy = nx // 2, ny // 2
    keys = message_keys(ngx, ngy)
    nk = len(keys)

    def dims(k, l, wx, lx, ly):
        return (lx if k is None else wx, ly if l is None else YW, cz)

    def send(some, arrays, hop):
        return [lax.ppermute(v, AXES, routes(sizes, k, l, hop)) for (k, l), v in zip(some, arrays)]

    def edge(v, l):
        first = jnp.where(upper("gy", l), v.shape[-2] - YW, 0)
        return lax.dynamic_slice_in_dim(v, first, YW, axis=v.ndim - 2)

    now = [(k, l) for k, l in keys if k is None or l != 0]
    after = [(k, l) for k, l in keys if k is not None and l == 0]
    straight = [(k, l) for k, l in now if l != 0]

    picks = tile_kinds[:, :, None] == jnp.arange(diffusivities.shape[0], dtype=jnp.int32)
    table = jnp.sum(jnp.where(picks, diffusivities, 0.0), axis=-1)
    local = table.shape
    table = jnp.pad(table, ((0, -local[0] % 8), (0, 128 - local[1])))
    tp = table.shape[0]

    def fine_dims(k, l):
        a, b, c = dims(k, l, FW, nx, ny)
        return shape(nodes * a + table_rows(b, tp), b, c)

    packed = pl.pallas_call(
        functools.partial(pack_kernel, keys),
        out_shape=[fine_dims(k, l) for k, l in keys],
        in_specs=[ANY, ANY],
        out_specs=[ANY] * nk,
        scratch_shapes=[pltpu.SemaphoreType.DMA((nk * (3 + tp),))],
        compiler_params=params(4),
        name="pack",
    )(u, table)
    halos = send(keys, packed, None)

    fye, cye, cxe = ny + 2 * YW, cy + 2 * YW, cx + 2 * CW + 4
    xe = nx + 2 * FW
    buf = pltpu.VMEM((xe, fye, cz), f32)
    depth = 2 * CW + 2 * CN
    seams = seam_count(ngx)
    ykeys = [key for key in keys if key[0] is None]
    yhalos = [m for key, m in zip(keys, halos) if key[0] is None]
    inner = pl.pallas_call(
        functools.partial(inner_kernel, ykeys, local, seams),
        out_shape=[
            shape(nx, ny, cz), shape(nx, ny, cz), shape(5, cx, cy, cz), shape(seams, FIELDS, FW + SEAM, fye, cz)
        ],
        in_specs=[SM, ANY, ANY] + [ANY] * len(ykeys),
        out_specs=[VM] * 4,
        scratch_shapes=[pltpu.VMEM((3, xe, fye, cz), f32)] + [buf] * 7
        + [
            pltpu.VMEM((3, xe // TILE, fye, cz), f32),
            pltpu.VMEM((3, 3, tp, cz), f32),
            pltpu.VMEM((5, fye // 2, cz), f32),
            pltpu.VMEM((4, fye, cz), f32),
            pltpu.SemaphoreType.DMA((nk * (3 + tp) + 2,)),
        ],
        compiler_params=params(38),
        cost_estimate=pl.CostEstimate(flops=200 * nx * ny * cz, bytes_accessed=40_000_000, transcendentals=0),
        name="fine_inner",
    )(section_steps, u, table, *yhalos)
    out = pl.pallas_call(
        functools.partial(seam_kernel, keys, now, local, seams),
        out_shape=[shape(*v.shape) for v in inner] + [shape(3, 3, tp, cz)]
        + [shape(*dims(k, l, depth, 4 * cx, cy)) for k, l in now],
        in_specs=[SM, ANY] + [ANY] * nk + [VM] * 4,
        out_specs=[VM] * (5 + len(now)),
        scratch_shapes=[
            pltpu.VMEM((seams, 3, FW, fye, cz), f32),
            pltpu.VMEM((3, (FW + SEAM) // TILE, fye, cz), f32),
            pltpu.VMEM((5, fye // 2, cz), f32),
            pltpu.VMEM((4, fye, cz), f32),
            pltpu.SemaphoreType.DMA((nk * (3 + tp) + 2,)),
        ],
        input_output_aliases={2 + nk + i: i for i in range(4)},
        compiler_params=params(24),
        name="fine_seam",
    )(section_steps, table, *halos, *inner)
    w1, w2, co, _, tables = out[:5]
    strips = dict(zip(now, lax.optimization_barrier(send(now, out[5:], None))))
    arrived = lax.ppermute(w2, "tm", [(i, i + 1) for i in range(nt - 1)])
    coef = pl.pallas_call(
        functools.partial(coarse_coefficient_kernel, local),
        out_shape=shape(2, cxe // 2, cye, cz),
        in_specs=[SM, VM],
        out_specs=VM,
        scratch_shapes=[pltpu.VMEM((4, cye, cz), f32)],
        compiler_params=params(4),
        name="coarse_coefficients",
    )(section_steps, tables)
    strips.update(zip(after, send([(None, l) for _, l in after], [edge(strips[(k, None)], l) for k, l in after], None)))

    ncopy = 4 + 4 * nk
    ge, ce = pl.pallas_call(
        functools.partial(assemble_kernel, keys),
        out_shape=[shape(3, cxe, cye, cz), shape(cxe, cye, cz)],
        in_specs=[ANY] + [ANY] * nk,
        out_specs=[VM, VM],
        scratch_shapes=[pltpu.VMEM((3, cxe, cye, cz), f32), pltpu.SemaphoreType.DMA((ncopy,))],
        compiler_params=params(10),
        name="assemble",
    )(co, *[strips[k] for k in keys])

    state, handed = None, None
    cbuf = pltpu.VMEM((cxe, cye, cz), f32)
    arrive = straight + [(None, 0)] * (0 in colors(ngy)) + after
    for n in range(nt):
        last = n == nt - 1
        args = [section_steps, ge, coef, co]
        specs = [SM, VM, VM, VM]
        alias = {}
        if n == 0:
            args.append(ce)
            specs.append(VM)
        else:
            alias = {len(args): 0}
            args += [state] + handed
            specs += [VM] + [ANY] * len(handed)
            if n == 1:
                args.append(arrived)
                specs.append(ANY)
        sent = [] if last else straight
        res = pl.pallas_call(
            functools.partial(chain_kernel, n, sent, arrive),
            out_shape=[shape(3, cx, cy, cz), shape(cx, cy, cz)] + [shape(*dims(k, l, CW, cx, cy)) for k, l in sent],
            in_specs=specs,
            out_specs=[VM] * (2 + len(sent)),
            scratch_shapes=[cbuf] * 4 + [pltpu.VMEM((2, cxe, cye, cz), f32), pltpu.SemaphoreType.DMA((nk + 1,))],
            input_output_aliases=alias,
            compiler_params=params(14),
            name=f"chain_{n}",
        )(*args)
        state = res[0]
        if not last:
            own = lax.ppermute(res[1], AXES, routes(sizes, None, None, n))
            own, *got = lax.optimization_barrier([own] + send(straight, res[2:], n))
            rows = [own] + [got[straight.index((k, None))] for k in colors(ngx)]
            side = []
            for l in colors(ngy)[:1]:
                strip = edge(jnp.concatenate(rows, axis=0), l)
                strip = lax.ppermute(strip, AXES, [p for p in routes(sizes, None, l, None) if p[1] // (ngx * ngy) == n + 1])
                side = [strip[:cx]] + [strip[cx + i * CW : cx + i * CW + CW] for i in range(len(after))]
            handed = [own] + got + side

    blk = 8
    fspec = pl.BlockSpec((blk, ny, cz), lambda i: (i, 0, 0))
    result = pl.pallas_call(
        finish_kernel,
        grid=(nx // blk,),
        out_shape=shape(3, nx, ny, cz),
        in_specs=[pl.BlockSpec((None, blk, ny, cz), lambda i: (0, i, 0, 0))] + [fspec] * 3
        + [pl.BlockSpec((3, blk // 2, cy, cz), lambda i: (0, i, 0, 0)), pl.BlockSpec((5, blk // 2, cy, cz), lambda i: (0, i, 0, 0))],
        out_specs=pl.BlockSpec((3, blk, ny, cz), lambda i: (0, i, 0, 0)),
        compiler_params=params(12),
        name="finish",
    )(u, arrived, w1, w2, state, co)
    return result[None]


def solution(mesh):
    sizes = tuple(mesh.shape[a] for a in AXES)
    return jax.shard_map(
        functools.partial(per_device, sizes),
        mesh=mesh,
        in_specs=(P("tm", None, "gx", "gy", None), P(), P(), P("gx", "gy")),
        out_specs=P("tm", None, "gx", "gy", None),
        check_vma=False,
    )
```

```python
import functools
import jax
import jax.numpy as jnp
from jax import lax
from jax.experimental import pallas as pl
from jax.experimental.pallas import tpu as pltpu
from jax.sharding import PartitionSpec as P

TILE = 4
FW = 8
CW = 6
CN = 3
SUB = 1
FEW, MANY, LOW = 8, 8, 6
YW = 8
STEP_UNIT = 0.05
WEIGHTS = ((5.0 / 24.0, 1.0 / 3.0, -1.0 / 24.0), (-1.0 / 24.0, 1.0 / 3.0, 5.0 / 24.0))
AXES = ("tm", "gx", "gy")
ANY = pl.BlockSpec(memory_space=pl.ANY)
VM = pl.BlockSpec(memory_space=pltpu.VMEM)
SM = pl.BlockSpec(memory_space=pltpu.SMEM)
f32 = jnp.float32


def params(mib):
    return pltpu.CompilerParams(vmem_limit_bytes=mib * 1024 * 1024)


def shape(*dims):
    return jax.ShapeDtypeStruct(dims, f32)


def partner(i, color, size):
    j = i + 1 if (i + color) % 2 == 0 else i - 1
    return j if 0 <= j < size else None


def colors(size):
    return [k for k in (0, 1) if any(partner(i, k, size) is not None for i in range(size))]


def routes(sizes, cx, cy, hop):
    nt, nx, ny = sizes
    out = []
    for t in range(nt):
        if hop is not None and t != hop:
            continue
        for x in range(nx):
            px = x if cx is None else partner(x, cx, nx)
            for y in range(ny):
                py = y if cy is None else partner(y, cy, ny)
                if px is None or py is None:
                    continue
                target = t if hop is None else t + 1
                out.append(((t * nx + px) * ny + py, (target * nx + x) * ny + y))
    return out


def message_keys(nx, ny):
    keys = [(k, None) for k in colors(nx)]
    keys += [(k, l) for k in colors(nx) for l in colors(ny)]
    keys += [(None, l) for l in colors(ny)]
    return keys


def upper(axis, color):
    return lax.rem(lax.axis_index(axis) + color, 2) == 0


def pick(cond, a, b):
    return jnp.where(cond, jnp.int32(a), jnp.int32(b))


def times(steps, sect):
    h = steps[sect].astype(f32) * STEP_UNIT
    return h, 0.5 * h


def reaction(v):
    return v - v * v * v


def run_copies(pairs, sems):
    copies = [pltpu.make_async_copy(a, b, sems.at[i]) for i, (a, b) in enumerate(pairs)]
    for c in copies:
        c.start()
    for c in copies:
        c.wait()


def table_rows(rows, tiles):
    return -(-tiles // rows)


def table_copies(table, msg, base, out):
    tiles, height = table.shape[0], msg.shape[1]
    pairs = []
    for i in range(table_rows(height, tiles)):
        n = min(height, tiles - i * height)
        pair = (table.at[pl.ds(i * height, n)], msg.at[base + i, pl.ds(0, n)])
        pairs.append(pair if out else pair[::-1])
    return pairs


def pack_kernel(keys, u, table, *rest):
    outs, sems = rest[:-1], rest[-1]
    nx, ny = u.shape[1], u.shape[2]
    pairs = []
    for (k, l), o in zip(keys, outs):
        w = nx if k is None else FW
        xs = pl.ds(0 if k is None else pick(upper("gx", k), nx - FW, 0), w)
        ys = pl.ds(0, ny) if l is None else pl.ds(pl.multiple_of(pick(upper("gy", l), ny - YW, 0), 8), YW)
        pairs += [(u.at[j, xs, ys, :], o.at[pl.ds(j * w, w)]) for j in range(3)]
        pairs += table_copies(table, o, 3 * w, True)
    run_copies(pairs, sems)


def permuted(ref, *lead):
    t_count = ref.shape[-2] // 8
    return jnp.concatenate([ref[(*lead, pl.ds(t, 8, stride=t_count))] for t in range(t_count)], axis=-2)


def store_plain(ref, lead, value):
    t_count = value.shape[-2] // 8
    for t in range(t_count):
        ref[(*lead, pl.ds(t, 8, stride=t_count))] = value[..., t * 8 : t * 8 + 8, :]


def expand(tables, tx, ty, row, piece, cells):
    sub = lax.broadcasted_iota(jnp.int32, (8, 128), 0)
    lane = lax.broadcasted_iota(jnp.int32, (8, 128), 1)
    if isinstance(row, int):
        sx = 0 if row < 0 else (2 if row >= tx else 1)
        r = row - (sx - 1) * tx
    else:
        sx = jnp.where(row < 0, 0, jnp.where(row >= tx, 2, 1))
        r = row - (sx - 1) * tx
    runs = ty * cells // 8
    per = 8 // cells
    sy, first = (0, ty - per) if piece < 0 else ((2, 0) if piece >= runs else (1, piece * per))
    hot = lane == first + lax.div(sub, cells)
    return jnp.sum(jnp.where(hot, tables[sx, sy, pl.ds(r, 1), :], 0.0), axis=1, keepdims=True)


def fill_coefficients(tables, local, cells, low, rows, plain, write):
    tx, ty = local
    count = plain.shape[1] // 8
    for i in range(rows):
        slot = i % plain.shape[0]
        for p in range(count):
            k = expand(tables, tx, ty, low + i, p - 1, cells)
            plain[slot, p * 8 : p * 8 + 8, :] = jnp.broadcast_to(k, (8, 128))
        write(i, jnp.concatenate([plain[slot, pl.ds(t, 8, stride=count), :] for t in range(count)], axis=0))


def coarse_coefficient_kernel(local, steps, tables, coarse, plain):
    _, a = times(steps, lax.axis_index("tm"))

    def write(i, k):
        inv = 1.0 / (1.0 + a * k * 3.0)
        coarse[0, i] = a * k * inv
        coarse[1, i] = inv

    rows = local[0] + CW
    fill_coefficients(tables, local, TILE // 2, -(CW // 2), rows, plain, write)
    for i in range(rows, coarse.shape[1]):
        write(i, jnp.zeros(plain.shape[1:], f32))


def neighbours(v, masks):
    c = v[1:-1]
    px = v[2:] + v[:-2]
    before = jnp.concatenate([pltpu.roll(c[:, -8:], 1, 1), c[:, :-8]], axis=1)
    after = jnp.concatenate([c[:, 8:], pltpu.roll(c[:, :8], 7, 1)], axis=1)
    z = pltpu.roll(c, 1, 2) * masks[0] + pltpu.roll(c, 127, 2) * masks[1]
    return c, px + (before + after), z


def z_masks():
    lane = lax.broadcasted_iota(jnp.int32, (1, 8, 128), 2)
    return (jnp.where(lane == 0, 0.0, 1.0), jnp.where(lane == 127, 0.0, 1.0))


def wide_masks(rows, y):
    return tuple(jnp.concatenate([jnp.concatenate([m] * (y // 8), axis=1)] * rows, axis=0) for m in z_masks())


def sweep_rows(own, width, r, step, body):
    gx, ngx = lax.axis_index("gx"), lax.axis_size("gx")
    n = own + r * min(ngx - 1, 2)
    pad = -n % step
    if ngx == 2:
        begin = width - pick(gx > 0, r, pad)
    else:
        begin = width - r * min(ngx - 1, 2) // 2
    lax.fori_loop(0, (n + pad) // step, lambda i, _: (body(begin + i * step), 0)[1], 0)


def clear_walls(width, own, bufs, count=CW):
    gx, ngx = lax.axis_index("gx"), lax.axis_size("gx")
    for b in bufs:
        zero = jnp.zeros((count,) + b.shape[1:], f32)

        @pl.when(gx == 0)
        def _():
            b[width - count : width] = zero

        @pl.when(gx == ngx - 1)
        def _():
            b[width + own : width + own + count] = zero


SEAM = 12
FIELDS = 10


class Stages:
    def __init__(self, u, f0, q0, qa, qb, p2, w1, w2, fine, h, a, tile_of):
        self.u, self.f0, self.q0, self.qa, self.qb, self.p2, self.w1, self.w2 = u, f0, q0, qa, qb, p2, w1, w2
        self.fine, self.h, self.a, self.tile_of = fine, h, a, tile_of

    def coef(self, n, x, step):
        return jnp.stack([self.fine[n, self.tile_of(x + i)] for i in range(step)])

    def forces(self, x, step, masks):
        k, h, a = self.coef(0, x, step), self.h, self.a
        c, f = [], []
        for j in range(3):
            cj, pj, zj = neighbours(self.u(j, pl.ds(x - 1, step + 2)), masks)
            c.append(cj)
            f.append(reaction(cj) + k * (pj + zj - 6.0 * cj))
        at = pl.ds(x, step)
        self.f0[at] = f[0]
        h0 = WEIGHTS[0][0] * f[0] + WEIGHTS[0][1] * f[1] + WEIGHTS[0][2] * f[2]
        h1 = WEIGHTS[1][0] * f[0] + WEIGHTS[1][1] * f[1] + WEIGHTS[1][2] * f[2]
        self.q0[at] = (c[0] + h * h0 - c[1]) * self.coef(2, x, step)
        self.p2[at] = h * h1 - c[2] - a * reaction(c[1])

    def jacobi(self, src, start, x, step, masks):
        _, p, z = neighbours(src[pl.ds(x - 1, step + 2)], masks)
        return start[pl.ds(x, step)] + self.coef(1, x, step) * (p + z)

    def into(self, dst, src, start):
        def body(x, step, masks):
            dst[pl.ds(x, step)] = self.jacobi(src, start, x, step, masks)
        return body

    def end1(self, x, step, masks):
        at = pl.ds(x, step)
        w = self.u(1, at) + self.jacobi(self.qb, self.q0, x, step, masks)
        self.w1[at] = w
        self.p2[at] = (w + self.a * reaction(w) + self.p2[at]) * self.coef(2, x, step)

    def end2(self, x, step, masks):
        at = pl.ds(x, step)
        self.w2[at] = self.u(2, at) + self.jacobi(self.qb, self.p2, x, step, masks)

    def bodies(self):
        return [
            (1, self.forces),
            (2, self.into(self.qa, self.q0, self.q0)),
            (3, self.into(self.qb, self.qa, self.q0)),
            (4, self.end1),
            (5, self.into(self.qa, self.p2, self.p2)),
            (6, self.into(self.qb, self.qa, self.p2)),
            (7, self.end2),
        ]

    def coarse_pair(self, x, i, w1o, w2o, co, plain, tmp, ny):
        ye = ny + 2 * YW
        masks = wide_masks(2, ye)
        h, a = self.h, self.a

        def pair_sum(v):
            v = v[0] + v[1]
            return jnp.concatenate([v[t : t + 8] + v[t + 8 : t + 16] for t in range(0, ye, 16)], axis=0)

        at = pl.ds(x, 2)
        k = self.coef(0, x, 2)
        g = [self.f0[at]]
        w = [self.u(0, at)]
        for m, (ref, out) in enumerate(((self.w1, w1o), (self.w2, w2o))):
            c, p, z = neighbours(ref[pl.ds(x - 1, 4)], masks)
            w.append(c)
            g.append(reaction(c) + k * (p + z - 6.0 * c))
            store_plain(tmp, (2 * m + 0,), c[0])
            store_plain(tmp, (2 * m + 1,), c[1])
            out[pl.ds(2 * i, 2)] = tmp[2 * m : 2 * m + 2, YW : YW + ny]
        c0, c1 = [pair_sum(wt[0] * g[0] + wt[1] * g[1] + wt[2] * g[2]) * 0.25 for wt in WEIGHTS]
        u0, u1, u2 = [pair_sum(v) * 0.25 for v in w]
        start = jnp.where(lax.axis_index("tm") == 0, u0 + a * reaction(u0), 0.0)
        values = (start + h * c0 - a * reaction(u0) - u1, u1, h * c1 - a * reaction(u1) - u2, u0, u2)
        for n, v in enumerate(values):
            store_plain(plain, (n,), v)
            co[n, i] = plain[n, YW // 2 : YW // 2 + ny // 2]


def parts(body, step, masks, x):
    for i in range(0, step, SUB):
        body(x + i, SUB, masks)


def seam_count(size):
    return min(size - 1, 2)


def seam_is_low(seam):
    return lax.axis_index("gx") > 0 if lax.axis_size("gx") == 2 else seam == 0


def target_y(l, ny):
    return pl.ds(YW, ny) if l is None else pl.ds(pl.multiple_of(pick(upper("gy", l), YW + ny, 0), 8), YW)


def inner_kernel(keys, local, seams, steps, u, table, *rest):
    nmsg = len(keys)
    msgs, rest = rest[:nmsg], rest[nmsg:]
    w1o, w2o, co, seam, rest = rest[0], rest[1], rest[2], rest[3], rest[4:]
    ue, f0, q0, qa, qb, p2, w1, w2, fine, tables, plain, tmp, sems = rest
    nx, ny = u.shape[1], u.shape[2]
    ye = ny + 2 * YW
    h, a = times(steps, lax.axis_index("tm"))

    if nmsg < 2:
        def clear(i, _):
            for j in range(3):
                ue[j, i] = jnp.zeros((ye, 128), f32)
            return 0
        lax.fori_loop(0, ue.shape[1], clear, 0)
    clear_walls(FW, nx, [ue.at[0], ue.at[1], ue.at[2], q0, qa, qb, p2, w1, w2], FW)
    for j in (0, 2):
        tables[1, j] = jnp.zeros(tables.shape[2:], f32)
    pairs = [(u, ue.at[:, pl.ds(FW, nx), pl.ds(YW, ny), :])]
    for (_, l), m in zip(keys, msgs):
        pairs += [(m.at[pl.ds(j * nx, nx)], ue.at[j, pl.ds(FW, nx), target_y(l, ny), :]) for j in range(3)]
        pairs += table_copies(tables.at[1, pick(upper("gy", l), 2, 0)], m, 3 * nx, False)
    pairs.append((table, tables.at[1, 1]))
    run_copies(pairs, sems)

    def write(i, k):
        inv = 1.0 / (1.0 + a * k * 6.0)
        fine[0, i] = k
        fine[1, i] = a * k * inv
        fine[2, i] = inv

    ft = FW // TILE
    for i in list(range(ft)) + list(range(ft + local[0], fine.shape[1])):
        write(i, jnp.zeros((ye, 128), f32))
    fill_coefficients(tables, local, TILE, 0, local[0], tmp, lambda i, k: write(ft + i, k))
    st = Stages(
        lambda j, at: permuted(ue, j, at), f0, q0, qa, qb, p2, w1, w2, fine, h, a, lambda x: lax.div(x, TILE)
    )
    for k, body in st.bodies():
        step = FEW if k == 1 else MANY
        if seams == 2 and (nx - 2 * k) % step:
            step = 2
        sweep_rows(nx, FW, -k, step, functools.partial(parts, body, step, wide_masks(SUB, ye)))

    def coarse_rows(x):
        st.coarse_pair(x, lax.div(x - FW, 2), w1o, w2o, co, plain, tmp, ny)

    sweep_rows(nx, FW, -8, 2, coarse_rows)
    for n in range(seams):
        low = seam_is_low(n)
        src, dst = pick(low, FW, FW + nx - SEAM), pick(low, FW, 0)

        def keep(i, _):
            x, to = pl.ds(src + 4 * i, 4), pl.ds(dst + 4 * i, 4)
            for j in range(3):
                seam[n, j, to] = permuted(ue, j, x)
            for j, b in enumerate((f0, q0, qa, qb, p2, w1, w2)):
                seam[n, 3 + j, to] = b[x]
            return 0

        lax.fori_loop(0, SEAM // 4, keep, 0)


def seam_kernel(keys, ckeys, local, seams, steps, table, *rest):
    nmsg = len(keys)
    msgs, rest = rest[:nmsg], rest[nmsg + 4 :]
    w1o, w2o, co, seam, tables = rest[:5]
    nc = len(ckeys)
    couts, rest = rest[5 : 5 + nc], rest[5 + nc :]
    halo, fine, plain, tmp, sems = rest
    nx, ny = w1o.shape[0], w1o.shape[1]
    ye = ny + 2 * YW
    h, a = times(steps, lax.axis_index("tm"))
    for i in range(3):
        for j in range(3):
            if (i, j) != (1, 1):
                tables[i, j] = jnp.zeros(tables.shape[2:], f32)
    if len(colors(lax.axis_size("gy"))) < 2 or len(colors(lax.axis_size("gx"))) < min(seams, 2):
        halo[...] = jnp.zeros(halo.shape, f32)
    pairs = []
    for (k, l), m in zip(keys, msgs):
        w = nx if k is None else FW
        if k is not None:
            n = 0 if seams == 1 else pick(upper("gx", k), 1, 0)
            pairs += [(m.at[pl.ds(j * w, w)], halo.at[n, j, :, target_y(l, ny), :]) for j in range(3)]
        sx = 1 if k is None else pick(upper("gx", k), 2, 0)
        sy = 1 if l is None else pick(upper("gy", l), 2, 0)
        pairs += table_copies(tables.at[sx, sy], m, 3 * w, False)
    pairs.append((table, tables.at[1, 1]))
    run_copies(pairs, sems)
    tx = local[0]
    for n in range(seams):
        low = seam_is_low(n)

        def write(i, k):
            inv = 1.0 / (1.0 + a * k * 6.0)
            fine[0, i] = k
            fine[1, i] = a * k * inv
            fine[2, i] = inv

        fill_coefficients(
            tables, local, TILE, pick(low, -(FW // TILE), tx - SEAM // TILE), fine.shape[1], tmp, write
        )
        to = pick(low, 0, SEAM)
        for i in range(0, FW, 4):
            for j in range(3):
                seam[n, j, pl.ds(to + i, 4)] = permuted(halo, n, j, pl.ds(i, 4))
        st = Stages(
            lambda j, at: seam[n, j, at], *[seam.at[n, 3 + j] for j in range(7)], fine, h, a, lambda x: lax.div(x, TILE)
        )
        for k, body in st.bodies():
            step = FEW if k == 1 else MANY
            masks = wide_masks(SUB, ye)
            first = pick(low, k, SEAM - k)
            lax.fori_loop(0, 8 // step, lambda i, _: (parts(body, step, masks, first + i * step), 0)[1], 0)
        first = pick(low, FW, SEAM - 8)
        row = pick(low, 0, nx // 2 - 4)
        lax.fori_loop(
            0, 4, lambda i, _: (st.coarse_pair(first + 2 * i, row + i, w1o, w2o, co, plain, tmp, ny), 0)[1], 0
        )
    cx, cy = nx // 2, ny // 2
    fields = ((0, CW), (1, CN), (2, CN))
    for (k, l), o in zip(ckeys, couts):
        ys = pl.ds(0, cy) if l is None else pl.ds(pl.multiple_of(pick(upper("gy", l), cy - YW, 0), 8), YW)
        at = 0
        for fld, width in fields:
            if k is None:
                width, first = cx, 0
            else:
                first = pick(upper("gx", k), cx - width, 0)
            o[pl.ds(at, width)] = co[fld, pl.ds(first, width), ys, :]
            at += width


def assemble_kernel(keys, co, *rest):
    nm = len(keys)
    msgs, (gp, ge), sems = rest[:nm], rest[nm : nm + 2], rest[nm + 2]
    cx, cy = co.shape[1], co.shape[2]

    def clear(i, _):
        for f in range(3):
            ge[f, i] = jnp.zeros(ge.shape[2:], f32)
        return 0

    lax.fori_loop(0, ge.shape[1], clear, 0)
    fields = ((0, CW), (1, CN), (2, CN))
    pairs = []

    for f, _ in fields:
        pairs.append((co.at[f], ge.at[f].at[pl.ds(CW, cx), pl.ds(YW, cy), :]))
    for (k, l), m in zip(keys, msgs):
        ys = pl.ds(YW, cy) if l is None else pl.ds(pl.multiple_of(pick(upper("gy", l), YW + cy, 0), 8), YW)
        at = 0
        for f, width in fields:
            if k is None:
                width, first = cx, CW
            else:
                first = pick(upper("gx", k), CW + cx, CW - width)
            pairs.append((m.at[pl.ds(at, width)], ge.at[f].at[pl.ds(first, width), ys, :]))
            at += width
    run_copies(pairs, sems)

    def order(i, _):
        at = pl.ds(2 * i, 2)
        for f in range(3):
            gp[f, at] = permuted(ge, f, at)
        return 0

    lax.fori_loop(0, ge.shape[1] // 2, order, 0)


def chain_kernel(turn, keys, arrive, last, steps, ge, coef, co, *rest):
    first = turn == 0
    if not first:
        _, own, rest = rest[0], rest[1], rest[2:]
        nm = len(arrive)
        msgs, rest = rest[:nm], rest[nm:]
        if turn == 1:
            rest = rest[1:]
        if last:
            ready, rest = rest[0], rest[1:]
    state = rest[0]
    rest = rest[1:]
    no = len(keys)
    whole, couts, rest = rest[0], rest[1 : 1 + no], rest[1 + no :]
    if last:
        final, stage, finals = rest[0], rest[-2], rest[-1]
        rest = rest[1:-2]
    cin, q0, qa, qb, plain, sems = rest
    cx, cy = co.shape[1], co.shape[2]
    ye = cy + 2 * YW
    sect = lax.axis_index("tm")
    h, a = times(steps, sect)
    ngx, ngy = lax.axis_size("gx"), lax.axis_size("gy")

    @pl.when(sect == turn)
    def _():
        clear_walls(CW, cx, (q0, qa, qb))
        if not first:
            if len(colors(ngy)) < 2:
                cin[...] = jnp.zeros(cin.shape, f32)
            else:
                clear_walls(CW, cx, (cin,))
            pairs = [(own, cin.at[pl.ds(CW, cx), pl.ds(YW, cy), :])]
            for (k, l), m in zip(arrive, msgs):
                if k is None:
                    xs = pl.ds(CW, cx)
                else:
                    xs = pl.ds(pick(upper("gx", k), CW + cx, 0), CW)
                ys = pl.ds(YW, cy) if l is None else pl.ds(pl.multiple_of(pick(upper("gy", l), YW + cy, 0), 8), YW)
                pairs.append((m, cin.at[xs, ys, :]))
            run_copies(pairs, sems)
        step = 1
        masks = wide_masks(step, ye)

        def rows(r, body):
            sweep_rows(cx, CW, r, LOW, lambda x: [body(x + i) for i in range(0, LOW, step)])

        def coefs(n, x):
            return jnp.stack([coef[n, lax.div(x + i, 2)] for i in range(step)])

        def jacobi(src, x):
            _, p, z = neighbours(src[pl.ds(x - 1, step + 2)], masks)
            return q0[pl.ds(x, step)] + coefs(0, x) * (0.25 * p + z)

        def into(dst, src):
            def body(x):
                dst[pl.ds(x, step)] = jacobi(src, x)
            return body

        def start(x):
            at = pl.ds(x, step)
            r = ge[0, at]
            if not first:
                v = permuted(cin, at)
                r = v + a * reaction(v) + r
            q0[at] = r * coefs(1, x)

        rows(6, start)
        rows(5, into(qa, q0))
        rows(4, into(qb, qa))

        def middle(x):
            at = pl.ds(x, step)
            w = ge[1, at] + jacobi(qb, x)
            q0[at] = (w + a * reaction(w) + ge[2, at]) * coefs(1, x)
            store_plain(plain, (0, at), w)

        rows(3, middle)
        rows(2, into(qa, q0))
        rows(1, into(qb, qa))

        def end(x):
            store_plain(plain, (1, pl.ds(x, step)), jacobi(qb, x))

        rows(0, end)

        def keep(i, _):
            x, at = pl.ds(CW + 4 * i, 4), pl.ds(4 * i, 4)
            state[0, at] = co[3, at] if first else cin[x, YW : YW + cy]
            state[1, at] = plain[0, x, YW : YW + cy]
            state[2, at] = co[4, at] + plain[1, x, YW : YW + cy]
            whole[at] = state[2, at]
            return 0

        lax.fori_loop(0, cx // 4, keep, 0)
        for (k, l), o in zip(keys, couts):
            xs = pl.ds(0, cx) if k is None else pl.ds(pick(upper("gx", k), cx - CW, 0), CW)
            ys = pl.ds(0, cy) if l is None else pl.ds(pl.multiple_of(pick(upper("gy", l), cy - YW, 0), 8), YW)
            o[...] = state[2, xs, ys, :]

    if last:
        correct(ready, state, final, stage, finals)


PIECES = 4


def prepare_kernel(u, arrived, early, w1, w2, co, _, ready, u0, sems):
    run_copies([(u.at[0], u0)], sems)
    sect = lax.axis_index("tm")
    ny = u0.shape[1]
    ft, ct = ny // 8, ny // 16

    def row(i, _):
        at = pl.ds(2 * i, 2)

        def fine_tile(ref, t):
            return ref[at, pl.ds(t, 8, stride=ft), :]

        for t in range(ct):
            base = []
            for d in range(2):
                came = jnp.where(sect == 1, fine_tile(early, 2 * t + d), fine_tile(arrived, 2 * t + d))
                base.append(jnp.where(sect == 0, fine_tile(u0, 2 * t + d), came))
            both = base[0] + base[1]
            less = ((both[0] + both[1]) * 0.25,) + tuple(co[n, i, pl.ds(t, 8, stride=ct), :] for n in (1, 4))
            for d in range(2):
                to = pl.ds(2 * t + d, 8, stride=ft)
                ready[0, at, to, :] = base[d] - less[0]
                ready[1, at, to, :] = fine_tile(w1, 2 * t + d) - less[1]
                ready[2, at, to, :] = fine_tile(w2, 2 * t + d) - less[2]
        return 0

    lax.fori_loop(0, u0.shape[0] // 2, row, 0)


def correct(ready, state, out, stage, sems):
    nx, ny = ready.shape[1], ready.shape[2]
    ft, ct = ny // 8, ny // 16
    rows = nx // PIECES
    copies = []
    for m in range(3):
        for p in range(PIECES):

            def row(i, _):
                at = pl.ds(2 * i, 2)
                for t in range(ct):
                    c = state[m, i, pl.ds(t, 8, stride=ct), :]
                    for d in range(2):
                        to = pl.ds(2 * t + d, 8, stride=ft)
                        stage[m, at, to, :] = ready[m, at, to, :] + c
                return 0

            lax.fori_loop(p * rows // 2, (p + 1) * rows // 2, row, 0)
            part = pl.ds(p * rows, rows)
            copies.append(pltpu.make_async_copy(stage.at[m, part], out.at[m, part], sems.at[m * PIECES + p]))
            copies[-1].start()
    for c in copies:
        c.wait()


def per_device(sizes, fine_nodes, section_steps, diffusivities, tile_kinds):
    nt, ngx, ngy = sizes
    u = fine_nodes[0]
    nodes, nx, ny, cz = u.shape
    cx, cy = nx // 2, ny // 2
    keys = message_keys(ngx, ngy)
    nk = len(keys)

    def dims(k, l, wx, lx, ly):
        return (lx if k is None else wx, ly if l is None else YW, cz)

    def send(some, arrays, hop):
        return [lax.ppermute(v, AXES, routes(sizes, k, l, hop)) for (k, l), v in zip(some, arrays)]

    def edge(v, l):
        first = jnp.where(upper("gy", l), v.shape[-2] - YW, 0)
        return lax.dynamic_slice_in_dim(v, first, YW, axis=v.ndim - 2)

    now = [(k, l) for k, l in keys if k is None or l != 0]
    after = [(k, l) for k, l in keys if k is not None and l == 0]
    straight = [(k, l) for k, l in now if l != 0]

    picks = tile_kinds[:, :, None] == jnp.arange(diffusivities.shape[0], dtype=jnp.int32)
    table = jnp.sum(jnp.where(picks, diffusivities, 0.0), axis=-1)
    local = table.shape
    table = jnp.pad(table, ((0, -local[0] % 8), (0, 128 - local[1])))
    tp = table.shape[0]

    def fine_dims(k, l):
        a, b, c = dims(k, l, FW, nx, ny)
        return shape(nodes * a + table_rows(b, tp), b, c)

    packed = pl.pallas_call(
        functools.partial(pack_kernel, keys),
        out_shape=[fine_dims(k, l) for k, l in keys],
        in_specs=[ANY, ANY],
        out_specs=[ANY] * nk,
        scratch_shapes=[pltpu.SemaphoreType.DMA((nk * (3 + tp),))],
        compiler_params=params(4),
        name="pack",
    )(u, table)
    halos = send(keys, packed, None)

    fye, cye, cxe = ny + 2 * YW, cy + 2 * YW, cx + 2 * CW + 4
    xe = nx + 2 * FW
    buf = pltpu.VMEM((xe, fye, cz), f32)
    depth = CW + 2 * CN
    seams = seam_count(ngx)
    ykeys = [key for key in keys if key[0] is None]
    yhalos = [m for key, m in zip(keys, halos) if key[0] is None]
    inner = pl.pallas_call(
        functools.partial(inner_kernel, ykeys, local, seams),
        out_shape=[
            shape(nx, ny, cz), shape(nx, ny, cz), shape(5, cx, cy, cz), shape(seams, FIELDS, FW + SEAM, fye, cz)
        ],
        in_specs=[SM, ANY, ANY] + [ANY] * len(ykeys),
        out_specs=[VM] * 4,
        scratch_shapes=[pltpu.VMEM((3, xe, fye, cz), f32)] + [buf] * 7
        + [
            pltpu.VMEM((3, xe // TILE, fye, cz), f32),
            pltpu.VMEM((3, 3, tp, cz), f32),
            pltpu.VMEM((5, fye // 2, cz), f32),
            pltpu.VMEM((4, fye, cz), f32),
            pltpu.SemaphoreType.DMA((nk * (3 + tp) + 2,)),
        ],
        compiler_params=params(38),
        cost_estimate=pl.CostEstimate(flops=200 * nx * ny * cz, bytes_accessed=40_000_000, transcendentals=0),
        name="fine_inner",
    )(section_steps, u, table, *yhalos)
    out = pl.pallas_call(
        functools.partial(seam_kernel, keys, now, local, seams),
        out_shape=[shape(*v.shape) for v in inner] + [shape(3, 3, tp, cz)]
        + [shape(*dims(k, l, depth, 3 * cx, cy)) for k, l in now],
        in_specs=[SM, ANY] + [ANY] * nk + [VM] * 4,
        out_specs=[VM] * (5 + len(now)),
        scratch_shapes=[
            pltpu.VMEM((seams, 3, FW, fye, cz), f32),
            pltpu.VMEM((3, (FW + SEAM) // TILE, fye, cz), f32),
            pltpu.VMEM((5, fye // 2, cz), f32),
            pltpu.VMEM((4, fye, cz), f32),
            pltpu.SemaphoreType.DMA((nk * (3 + tp) + 2,)),
        ],
        input_output_aliases={2 + nk + i: i for i in range(4)},
        compiler_params=params(24),
        name="fine_seam",
    )(section_steps, table, *halos, *inner)
    w1, w2, co, _, tables = out[:5]
    strips = dict(zip(now, lax.optimization_barrier(send(now, out[5:], None))))
    arrived = lax.ppermute(w2, "tm", [(i, i + 1) for i in range(1, nt - 1)])
    coef = pl.pallas_call(
        functools.partial(coarse_coefficient_kernel, local),
        out_shape=shape(2, cxe // 2, cye, cz),
        in_specs=[SM, VM],
        out_specs=VM,
        scratch_shapes=[pltpu.VMEM((4, cye, cz), f32)],
        compiler_params=params(4),
        name="coarse_coefficients",
    )(section_steps, tables)
    strips.update(zip(after, send([(None, l) for _, l in after], [edge(strips[(k, None)], l) for k, l in after], None)))

    ncopy = 3 + 3 * nk
    ge = pl.pallas_call(
        functools.partial(assemble_kernel, keys),
        out_shape=shape(3, cxe, cye, cz),
        in_specs=[ANY] + [ANY] * nk,
        out_specs=VM,
        scratch_shapes=[pltpu.VMEM((3, cxe, cye, cz), f32), pltpu.SemaphoreType.DMA((ncopy,))],
        compiler_params=params(10),
        name="assemble",
    )(co, *[strips[k] for k in keys])

    state, handed = None, None
    cbuf = pltpu.VMEM((cxe, cye, cz), f32)
    arrive = straight + [(None, 0)] * (0 in colors(ngy)) + after
    for n in range(nt):
        last = n == nt - 1
        args = [section_steps, ge, coef, co]
        specs = [SM, VM, VM, VM]
        alias = {}
        if n > 0:
            alias = {len(args): 0}
            args += [state] + handed
            specs += [VM] + [ANY] * len(handed)
            if n == 1:
                args.append(arrived)
                specs.append(ANY)
        sent = [] if last else straight
        outs = [shape(3, cx, cy, cz), shape(cx, cy, cz)] + [shape(*dims(k, l, CW, cx, cy)) for k, l in sent]
        ospecs = [VM] * len(outs)
        scratch = [cbuf] * 4 + [pltpu.VMEM((2, cxe, cye, cz), f32), pltpu.SemaphoreType.DMA((nk + 1,))]
        if last:
            args.append(ready)
            specs.append(VM)
            outs.append(shape(3, nx, ny, cz))
            ospecs.append(ANY)
            scratch += [pltpu.VMEM((3, nx, ny, cz), f32), pltpu.SemaphoreType.DMA((PIECES * 3,))]
        res = pl.pallas_call(
            functools.partial(chain_kernel, n, sent, arrive if n else [], last),
            out_shape=outs,
            in_specs=specs,
            out_specs=ospecs,
            scratch_shapes=scratch,
            input_output_aliases=alias,
            compiler_params=params(20 if last else 14),
            name=f"chain_{n}",
        )(*args)
        state = res[0]
        if not last:
            whole = res[1]
            own = lax.ppermute(whole, AXES, routes(sizes, None, None, n))
            moving = [own] + send(straight, res[2:], n)
            if n == nt - 2:
                ready = pl.pallas_call(
                    prepare_kernel,
                    out_shape=shape(3, nx, ny, cz),
                    in_specs=[ANY] + [VM] * 5 + [ANY],
                    out_specs=VM,
                    scratch_shapes=[pltpu.VMEM((nx, ny, cz), f32), pltpu.SemaphoreType.DMA((1,))],
                    compiler_params=params(16),
                    name="prepare",
                )(u, arrived, early, w1, w2, co, whole)
                moving.append(ready)
            moving = lax.optimization_barrier(moving)
            if n == min(1, nt - 2):
                late, moving[0] = lax.optimization_barrier((w2, moving[0]))
                early = lax.ppermute(late, "tm", [(0, 1)])
            own, got = moving[0], moving[1 : 1 + len(straight)]
            ready = moving[-1]
            rows = [own] + [got[straight.index((k, None))] for k in colors(ngx)]
            side = []
            for l in colors(ngy)[:1]:
                strip = edge(jnp.concatenate(rows, axis=0), l)
                pairs = [p for p in routes(sizes, None, l, None) if p[1] // (ngx * ngy) == n + 1]
                strip = lax.ppermute(strip, AXES, pairs)
                side = [strip[:cx]] + [strip[cx + i * CW : cx + i * CW + CW] for i in range(len(after))]
            handed = [own] + got + side
    return res[2][None]


def solution(mesh):
    sizes = tuple(mesh.shape[a] for a in AXES)
    return jax.shard_map(
        functools.partial(per_device, sizes),
        mesh=mesh,
        in_specs=(P("tm", None, "gx", "gy", None), P(), P(), P("gx", "gy")),
        out_specs=P("tm", None, "gx", "gy", None),
        check_vma=False,
    )
```

```python
import functools
import jax
import jax.numpy as jnp
from jax import lax
from jax.experimental import pallas as pl
from jax.experimental.pallas import tpu as pltpu
from jax.sharding import PartitionSpec as P

TILE = 4
FW = 8
CW = 6
CN = 3
SUB = 1
FEW, MANY, LOW = 8, 8, 6
YW = 8
STEP_UNIT = 0.05
WEIGHTS = ((5.0 / 24.0, 1.0 / 3.0, -1.0 / 24.0), (-1.0 / 24.0, 1.0 / 3.0, 5.0 / 24.0))
AXES = ("tm", "gx", "gy")
ANY = pl.BlockSpec(memory_space=pl.ANY)
VM = pl.BlockSpec(memory_space=pltpu.VMEM)
SM = pl.BlockSpec(memory_space=pltpu.SMEM)
f32 = jnp.float32


def params(mib):
    return pltpu.CompilerParams(vmem_limit_bytes=mib * 1024 * 1024)


def shape(*dims):
    return jax.ShapeDtypeStruct(dims, f32)


def partner(i, color, size):
    j = i + 1 if (i + color) % 2 == 0 else i - 1
    return j if 0 <= j < size else None


def colors(size):
    return [k for k in (0, 1) if any(partner(i, k, size) is not None for i in range(size))]


def routes(sizes, cx, cy, hop):
    nt, nx, ny = sizes
    out = []
    for t in range(nt):
        if hop is not None and t != hop:
            continue
        for x in range(nx):
            px = x if cx is None else partner(x, cx, nx)
            for y in range(ny):
                py = y if cy is None else partner(y, cy, ny)
                if px is None or py is None:
                    continue
                target = t if hop is None else t + 1
                out.append(((t * nx + px) * ny + py, (target * nx + x) * ny + y))
    return out


def message_keys(nx, ny):
    keys = [(k, None) for k in colors(nx)]
    keys += [(k, l) for k in colors(nx) for l in colors(ny)]
    keys += [(None, l) for l in colors(ny)]
    return keys


def upper(axis, color):
    return lax.rem(lax.axis_index(axis) + color, 2) == 0


def pick(cond, a, b):
    return jnp.where(cond, jnp.int32(a), jnp.int32(b))


def times(steps, sect):
    h = steps[sect].astype(f32) * STEP_UNIT
    return h, 0.5 * h


def reaction(v):
    return v - v * v * v


def run_copies(pairs, sems):
    copies = [pltpu.make_async_copy(a, b, sems.at[i]) for i, (a, b) in enumerate(pairs)]
    for c in copies:
        c.start()
    for c in copies:
        c.wait()


def table_rows(rows, tiles):
    return -(-tiles // rows)


def table_copies(table, msg, base, out):
    tiles, height = table.shape[0], msg.shape[1]
    pairs = []
    for i in range(table_rows(height, tiles)):
        n = min(height, tiles - i * height)
        pair = (table.at[pl.ds(i * height, n)], msg.at[base + i, pl.ds(0, n)])
        pairs.append(pair if out else pair[::-1])
    return pairs


def pack_kernel(keys, u, table, *rest):
    outs, sems = rest[:-1], rest[-1]
    nx, ny = u.shape[1], u.shape[2]
    pairs = []
    for (k, l), o in zip(keys, outs):
        w = nx if k is None else FW
        xs = pl.ds(0 if k is None else pick(upper("gx", k), nx - FW, 0), w)
        ys = pl.ds(0, ny) if l is None else pl.ds(pl.multiple_of(pick(upper("gy", l), ny - YW, 0), 8), YW)
        pairs += [(u.at[j, xs, ys, :], o.at[pl.ds(j * w, w)]) for j in range(3)]
        pairs += table_copies(table, o, 3 * w, True)
    run_copies(pairs, sems)


def permuted(ref, *lead):
    t_count = ref.shape[-2] // 8
    return jnp.concatenate([ref[(*lead, pl.ds(t, 8, stride=t_count))] for t in range(t_count)], axis=-2)


def store_plain(ref, lead, value):
    t_count = value.shape[-2] // 8
    for t in range(t_count):
        ref[(*lead, pl.ds(t, 8, stride=t_count))] = value[..., t * 8 : t * 8 + 8, :]


def expand(tables, tx, ty, row, piece, cells):
    sub = lax.broadcasted_iota(jnp.int32, (8, 128), 0)
    lane = lax.broadcasted_iota(jnp.int32, (8, 128), 1)
    if isinstance(row, int):
        sx = 0 if row < 0 else (2 if row >= tx else 1)
        r = row - (sx - 1) * tx
    else:
        sx = jnp.where(row < 0, 0, jnp.where(row >= tx, 2, 1))
        r = row - (sx - 1) * tx
    runs = ty * cells // 8
    per = 8 // cells
    sy, first = (0, ty - per) if piece < 0 else ((2, 0) if piece >= runs else (1, piece * per))
    hot = lane == first + lax.div(sub, cells)
    return jnp.sum(jnp.where(hot, tables[sx, sy, pl.ds(r, 1), :], 0.0), axis=1, keepdims=True)


def fill_coefficients(tables, local, cells, low, rows, plain, write):
    tx, ty = local
    count = plain.shape[1] // 8
    for i in range(rows):
        slot = i % plain.shape[0]
        for p in range(count):
            k = expand(tables, tx, ty, low + i, p - 1, cells)
            plain[slot, p * 8 : p * 8 + 8, :] = jnp.broadcast_to(k, (8, 128))
        write(i, jnp.concatenate([plain[slot, pl.ds(t, 8, stride=count), :] for t in range(count)], axis=0))


def coarse_coefficient_kernel(local, steps, tables, coarse, plain):
    _, a = times(steps, lax.axis_index("tm"))

    def write(i, k):
        inv = 1.0 / (1.0 + a * k * 3.0)
        coarse[0, i] = a * k * inv
        coarse[1, i] = inv

    rows = local[0] + CW
    fill_coefficients(tables, local, TILE // 2, -(CW // 2), rows, plain, write)
    for i in range(rows, coarse.shape[1]):
        write(i, jnp.zeros(plain.shape[1:], f32))


def neighbours(v, masks):
    c = v[1:-1]
    px = v[2:] + v[:-2]
    before = jnp.concatenate([pltpu.roll(c[:, -8:], 1, 1), c[:, :-8]], axis=1)
    after = jnp.concatenate([c[:, 8:], pltpu.roll(c[:, :8], 7, 1)], axis=1)
    z = pltpu.roll(c, 1, 2) * masks[0] + pltpu.roll(c, 127, 2) * masks[1]
    return c, px + (before + after), z


def z_masks():
    lane = lax.broadcasted_iota(jnp.int32, (1, 8, 128), 2)
    return (jnp.where(lane == 0, 0.0, 1.0), jnp.where(lane == 127, 0.0, 1.0))


def wide_masks(rows, y):
    return tuple(jnp.concatenate([jnp.concatenate([m] * (y // 8), axis=1)] * rows, axis=0) for m in z_masks())


def sweep_rows(own, width, r, step, body):
    gx, ngx = lax.axis_index("gx"), lax.axis_size("gx")
    n = own + r * min(ngx - 1, 2)
    pad = -n % step
    if ngx == 2:
        begin = width - pick(gx > 0, r, pad)
    else:
        begin = width - r * min(ngx - 1, 2) // 2
    lax.fori_loop(0, (n + pad) // step, lambda i, _: (body(begin + i * step), 0)[1], 0)


def clear_walls(width, own, bufs, count=CW):
    gx, ngx = lax.axis_index("gx"), lax.axis_size("gx")
    for b in bufs:
        zero = jnp.zeros((count,) + b.shape[1:], f32)

        @pl.when(gx == 0)
        def _():
            b[width - count : width] = zero

        @pl.when(gx == ngx - 1)
        def _():
            b[width + own : width + own + count] = zero


SEAM = 12
FIELDS = 10


class Stages:
    def __init__(self, u, f0, q0, qa, qb, p2, w1, w2, fine, h, a, tile_of):
        self.u, self.f0, self.q0, self.qa, self.qb, self.p2, self.w1, self.w2 = u, f0, q0, qa, qb, p2, w1, w2
        self.fine, self.h, self.a, self.tile_of = fine, h, a, tile_of

    def coef(self, n, x, step):
        return jnp.stack([self.fine[n, self.tile_of(x + i)] for i in range(step)])

    def forces(self, x, step, masks):
        k, h, a = self.coef(0, x, step), self.h, self.a
        c, f = [], []
        for j in range(3):
            cj, pj, zj = neighbours(self.u(j, pl.ds(x - 1, step + 2)), masks)
            c.append(cj)
            f.append(reaction(cj) + k * (pj + zj - 6.0 * cj))
        at = pl.ds(x, step)
        self.f0[at] = f[0]
        h0 = WEIGHTS[0][0] * f[0] + WEIGHTS[0][1] * f[1] + WEIGHTS[0][2] * f[2]
        h1 = WEIGHTS[1][0] * f[0] + WEIGHTS[1][1] * f[1] + WEIGHTS[1][2] * f[2]
        self.q0[at] = (c[0] + h * h0 - c[1]) * self.coef(2, x, step)
        self.p2[at] = h * h1 - c[2] - a * reaction(c[1])

    def jacobi(self, src, start, x, step, masks):
        _, p, z = neighbours(src[pl.ds(x - 1, step + 2)], masks)
        return start[pl.ds(x, step)] + self.coef(1, x, step) * (p + z)

    def into(self, dst, src, start):
        def body(x, step, masks):
            dst[pl.ds(x, step)] = self.jacobi(src, start, x, step, masks)
        return body

    def end1(self, x, step, masks):
        at = pl.ds(x, step)
        w = self.u(1, at) + self.jacobi(self.qb, self.q0, x, step, masks)
        self.w1[at] = w
        self.p2[at] = (w + self.a * reaction(w) + self.p2[at]) * self.coef(2, x, step)

    def end2(self, x, step, masks):
        at = pl.ds(x, step)
        self.w2[at] = self.u(2, at) + self.jacobi(self.qb, self.p2, x, step, masks)

    def bodies(self):
        return [
            (1, self.forces),
            (2, self.into(self.qa, self.q0, self.q0)),
            (3, self.into(self.qb, self.qa, self.q0)),
            (4, self.end1),
            (5, self.into(self.qa, self.p2, self.p2)),
            (6, self.into(self.qb, self.qa, self.p2)),
            (7, self.end2),
        ]

    def coarse_pair(self, x, i, w1o, w2o, co, plain, tmp, ny, turn=0):
        ye = ny + 2 * YW
        masks = wide_masks(2, ye)
        h, a = self.h, self.a

        def pair_sum(v):
            v = v[0] + v[1]
            return jnp.concatenate([v[t : t + 8] + v[t + 8 : t + 16] for t in range(0, ye, 16)], axis=0)

        at = pl.ds(x, 2)
        k = self.coef(0, x, 2)
        g = [self.f0[at]]
        w = [self.u(0, at)]
        for m, (ref, out) in enumerate(((self.w1, w1o), (self.w2, w2o))):
            c, p, z = neighbours(ref[pl.ds(x - 1, 4)], masks)
            w.append(c)
            g.append(reaction(c) + k * (p + z - 6.0 * c))
            slot = 4 * turn + 2 * m
            store_plain(tmp, (slot,), c[0])
            store_plain(tmp, (slot + 1,), c[1])
            out[pl.ds(2 * i, 2)] = tmp[slot : slot + 2, YW : YW + ny]
        c0, c1 = [pair_sum(wt[0] * g[0] + wt[1] * g[1] + wt[2] * g[2]) * 0.25 for wt in WEIGHTS]
        u0, u1, u2 = [pair_sum(v) * 0.25 for v in w]
        start = jnp.where(lax.axis_index("tm") == 0, u0 + a * reaction(u0), 0.0)
        values = (start + h * c0 - a * reaction(u0) - u1, u1, h * c1 - a * reaction(u1) - u2, u0, u2)
        for n, v in enumerate(values):
            store_plain(plain, (5 * turn + n,), v)
            co[n, i] = plain[5 * turn + n, YW // 2 : YW // 2 + ny // 2]


def parts(body, step, masks, x):
    for i in range(0, step, SUB):
        body(x + i, SUB, masks)


def seam_count(size):
    return min(size - 1, 2)


def seam_is_low(seam):
    return lax.axis_index("gx") > 0 if lax.axis_size("gx") == 2 else seam == 0


def target_y(l, ny):
    return pl.ds(YW, ny) if l is None else pl.ds(pl.multiple_of(pick(upper("gy", l), YW + ny, 0), 8), YW)


def inner_kernel(keys, local, seams, steps, u, table, *rest):
    nmsg = len(keys)
    msgs, rest = rest[:nmsg], rest[nmsg:]
    w1o, w2o, co, seam, rest = rest[0], rest[1], rest[2], rest[3], rest[4:]
    ue, f0, q0, qa, qb, p2, w1, w2, fine, tables, plain, tmp, sems = rest
    nx, ny = u.shape[1], u.shape[2]
    ye = ny + 2 * YW
    h, a = times(steps, lax.axis_index("tm"))

    if nmsg < 2:
        def clear(i, _):
            for j in range(3):
                ue[j, i] = jnp.zeros((ye, 128), f32)
            return 0
        lax.fori_loop(0, ue.shape[1], clear, 0)
    clear_walls(FW, nx, [ue.at[0], ue.at[1], ue.at[2], q0, qa, qb, p2, w1, w2], FW)
    for j in (0, 2):
        tables[1, j] = jnp.zeros(tables.shape[2:], f32)
    pairs = [(u, ue.at[:, pl.ds(FW, nx), pl.ds(YW, ny), :])]
    for (_, l), m in zip(keys, msgs):
        pairs += [(m.at[pl.ds(j * nx, nx)], ue.at[j, pl.ds(FW, nx), target_y(l, ny), :]) for j in range(3)]
        pairs += table_copies(tables.at[1, pick(upper("gy", l), 2, 0)], m, 3 * nx, False)
    pairs.append((table, tables.at[1, 1]))
    run_copies(pairs, sems)

    def write(i, k):
        inv = 1.0 / (1.0 + a * k * 6.0)
        fine[0, i] = k
        fine[1, i] = a * k * inv
        fine[2, i] = inv

    ft = FW // TILE
    for i in list(range(ft)) + list(range(ft + local[0], fine.shape[1])):
        write(i, jnp.zeros((ye, 128), f32))
    fill_coefficients(tables, local, TILE, 0, local[0], tmp, lambda i, k: write(ft + i, k))
    st = Stages(
        lambda j, at: permuted(ue, j, at), f0, q0, qa, qb, p2, w1, w2, fine, h, a, lambda x: lax.div(x, TILE)
    )
    for k, body in st.bodies():
        n = nx - k * seams
        step = min((s for s in range(7, 33) if seams < 2 or n % s == 0), key=lambda s: (-n % s, -s), default=2)
        sweep_rows(nx, FW, -k, step, functools.partial(parts, body, step, wide_masks(SUB, ye)))

    def coarse_rows(x):
        for turn in range(2):
            y = x + 2 * turn
            st.coarse_pair(y, lax.div(y - FW, 2), w1o, w2o, co, plain, tmp, ny, turn)

    sweep_rows(nx, FW, -8, 4, coarse_rows)
    for n in range(seams):
        low = seam_is_low(n)
        src, dst = pick(low, FW, FW + nx - SEAM), pick(low, FW, 0)

        def keep(i, _):
            x, to = pl.ds(src + 4 * i, 4), pl.ds(dst + 4 * i, 4)
            for j in range(3):
                seam[n, j, to] = permuted(ue, j, x)
            for j, b in enumerate((f0, q0, qa, qb, p2, w1, w2)):
                seam[n, 3 + j, to] = b[x]
            return 0

        lax.fori_loop(0, SEAM // 4, keep, 0)


def seam_kernel(keys, ckeys, local, seams, steps, table, *rest):
    nmsg = len(keys)
    msgs, rest = rest[:nmsg], rest[nmsg + 4 :]
    w1o, w2o, co, seam, tables = rest[:5]
    nc = len(ckeys)
    couts, rest = rest[5 : 5 + nc], rest[5 + nc :]
    halo, fine, plain, tmp, sems = rest
    nx, ny = w1o.shape[0], w1o.shape[1]
    ye = ny + 2 * YW
    h, a = times(steps, lax.axis_index("tm"))
    for i in range(3):
        for j in range(3):
            if (i, j) != (1, 1):
                tables[i, j] = jnp.zeros(tables.shape[2:], f32)
    if len(colors(lax.axis_size("gy"))) < 2 or len(colors(lax.axis_size("gx"))) < min(seams, 2):
        halo[...] = jnp.zeros(halo.shape, f32)
    pairs = []
    for (k, l), m in zip(keys, msgs):
        w = nx if k is None else FW
        if k is not None:
            n = 0 if seams == 1 else pick(upper("gx", k), 1, 0)
            pairs += [(m.at[pl.ds(j * w, w)], halo.at[n, j, :, target_y(l, ny), :]) for j in range(3)]
        sx = 1 if k is None else pick(upper("gx", k), 2, 0)
        sy = 1 if l is None else pick(upper("gy", l), 2, 0)
        pairs += table_copies(tables.at[sx, sy], m, 3 * w, False)
    pairs.append((table, tables.at[1, 1]))
    run_copies(pairs, sems)
    tx = local[0]
    for n in range(seams):
        low = seam_is_low(n)

        def write(i, k):
            inv = 1.0 / (1.0 + a * k * 6.0)
            fine[0, i] = k
            fine[1, i] = a * k * inv
            fine[2, i] = inv

        fill_coefficients(
            tables, local, TILE, pick(low, -(FW // TILE), tx - SEAM // TILE), fine.shape[1], tmp, write
        )
        to = pick(low, 0, SEAM)
        for i in range(0, FW, 4):
            for j in range(3):
                seam[n, j, pl.ds(to + i, 4)] = permuted(halo, n, j, pl.ds(i, 4))
        st = Stages(
            lambda j, at: seam[n, j, at], *[seam.at[n, 3 + j] for j in range(7)], fine, h, a, lambda x: lax.div(x, TILE)
        )
        for k, body in st.bodies():
            step = FEW if k == 1 else MANY
            masks = wide_masks(SUB, ye)
            first = pick(low, k, SEAM - k)
            lax.fori_loop(0, 8 // step, lambda i, _: (parts(body, step, masks, first + i * step), 0)[1], 0)
        first = pick(low, FW, SEAM - 8)
        row = pick(low, 0, nx // 2 - 4)
        for i in range(4):
            st.coarse_pair(first + 2 * i, row + i, w1o, w2o, co, plain, tmp, ny, i % 2)
    cx, cy = nx // 2, ny // 2
    fields = ((0, CW), (1, CN), (2, CN))
    for (k, l), o in zip(ckeys, couts):
        ys = pl.ds(0, cy) if l is None else pl.ds(pl.multiple_of(pick(upper("gy", l), cy - YW, 0), 8), YW)
        at = 0
        for fld, width in fields:
            if k is None:
                width, first = cx, 0
            else:
                first = pick(upper("gx", k), cx - width, 0)
            o[pl.ds(at, width)] = co[fld, pl.ds(first, width), ys, :]
            at += width


def assemble_kernel(keys, co, *rest):
    nm = len(keys)
    msgs, (gp, ge), sems = rest[:nm], rest[nm : nm + 2], rest[nm + 2]
    cx, cy = co.shape[1], co.shape[2]

    def clear(i, _):
        for f in range(3):
            ge[f, i] = jnp.zeros(ge.shape[2:], f32)
        return 0

    lax.fori_loop(0, ge.shape[1], clear, 0)
    fields = ((0, CW), (1, CN), (2, CN))
    pairs = []

    for f, _ in fields:
        pairs.append((co.at[f], ge.at[f].at[pl.ds(CW, cx), pl.ds(YW, cy), :]))
    for (k, l), m in zip(keys, msgs):
        ys = pl.ds(YW, cy) if l is None else pl.ds(pl.multiple_of(pick(upper("gy", l), YW + cy, 0), 8), YW)
        at = 0
        for f, width in fields:
            if k is None:
                width, first = cx, CW
            else:
                first = pick(upper("gx", k), CW + cx, CW - width)
            pairs.append((m.at[pl.ds(at, width)], ge.at[f].at[pl.ds(first, width), ys, :]))
            at += width
    run_copies(pairs, sems)

    def order(i, _):
        at = pl.ds(2 * i, 2)
        for f in range(3):
            gp[f, at] = permuted(ge, f, at)
        return 0

    lax.fori_loop(0, ge.shape[1] // 2, order, 0)


def chain_kernel(turn, keys, arrive, last, steps, ge, coef, co, *rest):
    first = turn == 0
    if not first:
        _, own, rest = rest[0], rest[1], rest[2:]
        nm = len(arrive)
        msgs, rest = rest[:nm], rest[nm:]
        if turn == 1:
            rest = rest[1:]
        if last:
            ready, rest = rest[0], rest[1:]
    state = rest[0]
    rest = rest[1:]
    no = len(keys)
    whole, couts, rest = rest[0], rest[1 : 1 + no], rest[1 + no :]
    if last:
        final, stage, finals = rest[0], rest[-2], rest[-1]
        rest = rest[1:-2]
    cin, q0, qa, qb, plain, sems = rest
    cx, cy = co.shape[1], co.shape[2]
    ye = cy + 2 * YW
    sect = lax.axis_index("tm")
    h, a = times(steps, sect)
    ngx, ngy = lax.axis_size("gx"), lax.axis_size("gy")

    @pl.when(sect == turn)
    def _():
        clear_walls(CW, cx, (q0, qa, qb))
        if not first:
            if len(colors(ngy)) < 2:
                cin[...] = jnp.zeros(cin.shape, f32)
            else:
                clear_walls(CW, cx, (cin,))
            pairs = [(own, cin.at[pl.ds(CW, cx), pl.ds(YW, cy), :])]
            for (k, l), m in zip(arrive, msgs):
                if k is None:
                    xs = pl.ds(CW, cx)
                else:
                    xs = pl.ds(pick(upper("gx", k), CW + cx, 0), CW)
                ys = pl.ds(YW, cy) if l is None else pl.ds(pl.multiple_of(pick(upper("gy", l), YW + cy, 0), 8), YW)
                pairs.append((m, cin.at[xs, ys, :]))
            run_copies(pairs, sems)
        step = 1
        masks = wide_masks(step, ye)

        def rows(r, body):
            n = cx + r * min(ngx - 1, 2)
            sweep_rows(cx, CW, r, n, lambda x: [body(x + i) for i in range(0, n, step)])

        def coefs(n, x):
            return jnp.stack([coef[n, lax.div(x + i, 2)] for i in range(step)])

        def jacobi(src, x):
            _, p, z = neighbours(src[pl.ds(x - 1, step + 2)], masks)
            return q0[pl.ds(x, step)] + coefs(0, x) * (0.25 * p + z)

        def into(dst, src):
            def body(x):
                dst[pl.ds(x, step)] = jacobi(src, x)
            return body

        def start(x):
            at = pl.ds(x, step)
            r = ge[0, at]
            if not first:
                v = permuted(cin, at)
                r = v + a * reaction(v) + r
            q0[at] = r * coefs(1, x)

        rows(6, start)
        rows(5, into(qa, q0))
        rows(4, into(qb, qa))

        def middle(x):
            at = pl.ds(x, step)
            w = ge[1, at] + jacobi(qb, x)
            q0[at] = (w + a * reaction(w) + ge[2, at]) * coefs(1, x)
            store_plain(plain, (0, at), w)

        rows(3, middle)
        rows(2, into(qa, q0))
        rows(1, into(qb, qa))

        def end(x):
            store_plain(plain, (1, pl.ds(x, step)), jacobi(qb, x))

        rows(0, end)

        def keep(i, _):
            x, at = pl.ds(CW + 4 * i, 4), pl.ds(4 * i, 4)
            state[0, at] = co[3, at] if first else cin[x, YW : YW + cy]
            state[1, at] = plain[0, x, YW : YW + cy]
            state[2, at] = co[4, at] + plain[1, x, YW : YW + cy]
            whole[at] = state[2, at]
            return 0

        lax.fori_loop(0, cx // 4, keep, 0)
        for (k, l), o in zip(keys, couts):
            xs = pl.ds(0, cx) if k is None else pl.ds(pick(upper("gx", k), cx - CW, 0), CW)
            ys = pl.ds(0, cy) if l is None else pl.ds(pl.multiple_of(pick(upper("gy", l), cy - YW, 0), 8), YW)
            o[...] = state[2, xs, ys, :]

    if last:
        correct(ready, state, final, stage, finals)


PIECES = 4


def prepare_kernel(u, arrived, early, w1, w2, co, _, ready, u0, sems):
    run_copies([(u.at[0], u0)], sems)
    sect = lax.axis_index("tm")
    ny = u0.shape[1]
    ft, ct = ny // 8, ny // 16

    def row(i, _):
        at = pl.ds(2 * i, 2)

        def fine_tile(ref, t):
            return ref[at, pl.ds(t, 8, stride=ft), :]

        for t in range(ct):
            base = []
            for d in range(2):
                came = jnp.where(sect == 1, fine_tile(early, 2 * t + d), fine_tile(arrived, 2 * t + d))
                base.append(jnp.where(sect == 0, fine_tile(u0, 2 * t + d), came))
            both = base[0] + base[1]
            less = ((both[0] + both[1]) * 0.25,) + tuple(co[n, i, pl.ds(t, 8, stride=ct), :] for n in (1, 4))
            for d in range(2):
                to = pl.ds(2 * t + d, 8, stride=ft)
                ready[0, at, to, :] = base[d] - less[0]
                ready[1, at, to, :] = fine_tile(w1, 2 * t + d) - less[1]
                ready[2, at, to, :] = fine_tile(w2, 2 * t + d) - less[2]
        return 0

    lax.fori_loop(0, u0.shape[0] // 2, row, 0)


def correct(ready, state, out, stage, sems):
    nx, ny = ready.shape[1], ready.shape[2]
    ft, ct = ny // 8, ny // 16
    rows = nx // PIECES
    copies = []
    for m in range(3):
        for p in range(PIECES):

            def row(i, _):
                at = pl.ds(2 * i, 2)
                for t in range(ct):
                    c = state[m, i, pl.ds(t, 8, stride=ct), :]
                    for d in range(2):
                        to = pl.ds(2 * t + d, 8, stride=ft)
                        stage[m, at, to, :] = ready[m, at, to, :] + c
                return 0

            lax.fori_loop(p * rows // 2, (p + 1) * rows // 2, row, 0)
            part = pl.ds(p * rows, rows)
            copies.append(pltpu.make_async_copy(stage.at[m, part], out.at[m, part], sems.at[m * PIECES + p]))
            copies[-1].start()
    for c in copies:
        c.wait()


def per_device(sizes, fine_nodes, section_steps, diffusivities, tile_kinds):
    nt, ngx, ngy = sizes
    u = fine_nodes[0]
    nodes, nx, ny, cz = u.shape
    cx, cy = nx // 2, ny // 2
    keys = message_keys(ngx, ngy)
    nk = len(keys)

    def dims(k, l, wx, lx, ly):
        return (lx if k is None else wx, ly if l is None else YW, cz)

    def send(some, arrays, hop):
        return [lax.ppermute(v, AXES, routes(sizes, k, l, hop)) for (k, l), v in zip(some, arrays)]

    def edge(v, l):
        first = jnp.where(upper("gy", l), v.shape[-2] - YW, 0)
        return lax.dynamic_slice_in_dim(v, first, YW, axis=v.ndim - 2)

    now = [(k, l) for k, l in keys if k is None or l != 0]
    after = [(k, l) for k, l in keys if k is not None and l == 0]
    straight = [(k, l) for k, l in now if l != 0]

    picks = tile_kinds[:, :, None] == jnp.arange(diffusivities.shape[0], dtype=jnp.int32)
    table = jnp.sum(jnp.where(picks, diffusivities, 0.0), axis=-1)
    local = table.shape
    table = jnp.pad(table, ((0, -local[0] % 8), (0, 128 - local[1])))
    tp = table.shape[0]

    def fine_dims(k, l):
        a, b, c = dims(k, l, FW, nx, ny)
        return shape(nodes * a + table_rows(b, tp), b, c)

    packed = pl.pallas_call(
        functools.partial(pack_kernel, keys),
        out_shape=[fine_dims(k, l) for k, l in keys],
        in_specs=[ANY, ANY],
        out_specs=[ANY] * nk,
        scratch_shapes=[pltpu.SemaphoreType.DMA((nk * (3 + tp),))],
        compiler_params=params(4),
        name="pack",
    )(u, table)
    halos = send(keys, packed, None)

    fye, cye, cxe = ny + 2 * YW, cy + 2 * YW, cx + 2 * CW + 4
    xe = nx + 2 * FW
    buf = pltpu.VMEM((xe, fye, cz), f32)
    depth = CW + 2 * CN
    seams = seam_count(ngx)
    ykeys = [key for key in keys if key[0] is None]
    yhalos = [m for key, m in zip(keys, halos) if key[0] is None]
    inner = pl.pallas_call(
        functools.partial(inner_kernel, ykeys, local, seams),
        out_shape=[
            shape(nx, ny, cz), shape(nx, ny, cz), shape(5, cx, cy, cz), shape(seams, FIELDS, FW + SEAM, fye, cz)
        ],
        in_specs=[SM, ANY, ANY] + [ANY] * len(ykeys),
        out_specs=[VM] * 4,
        scratch_shapes=[pltpu.VMEM((3, xe, fye, cz), f32)] + [buf] * 7
        + [
            pltpu.VMEM((3, xe // TILE, fye, cz), f32),
            pltpu.VMEM((3, 3, tp, cz), f32),
            pltpu.VMEM((10, fye // 2, cz), f32),
            pltpu.VMEM((8, fye, cz), f32),
            pltpu.SemaphoreType.DMA((nk * (3 + tp) + 2,)),
        ],
        compiler_params=params(38),
        cost_estimate=pl.CostEstimate(flops=200 * nx * ny * cz, bytes_accessed=40_000_000, transcendentals=0),
        name="fine_inner",
    )(section_steps, u, table, *yhalos)
    out = pl.pallas_call(
        functools.partial(seam_kernel, keys, now, local, seams),
        out_shape=[shape(*v.shape) for v in inner] + [shape(3, 3, tp, cz)]
        + [shape(*dims(k, l, depth, 3 * cx, cy)) for k, l in now],
        in_specs=[SM, ANY] + [ANY] * nk + [VM] * 4,
        out_specs=[VM] * (5 + len(now)),
        scratch_shapes=[
            pltpu.VMEM((seams, 3, FW, fye, cz), f32),
            pltpu.VMEM((3, (FW + SEAM) // TILE, fye, cz), f32),
            pltpu.VMEM((10, fye // 2, cz), f32),
            pltpu.VMEM((8, fye, cz), f32),
            pltpu.SemaphoreType.DMA((nk * (3 + tp) + 2,)),
        ],
        input_output_aliases={2 + nk + i: i for i in range(4)},
        compiler_params=params(24),
        name="fine_seam",
    )(section_steps, table, *halos, *inner)
    w1, w2, co, _, tables = out[:5]
    strips = dict(zip(now, lax.optimization_barrier(send(now, out[5:], None))))
    arrived = lax.ppermute(w2, "tm", [(i, i + 1) for i in range(1, nt - 1)])
    coef = pl.pallas_call(
        functools.partial(coarse_coefficient_kernel, local),
        out_shape=shape(2, cxe // 2, cye, cz),
        in_specs=[SM, VM],
        out_specs=VM,
        scratch_shapes=[pltpu.VMEM((4, cye, cz), f32)],
        compiler_params=params(4),
        name="coarse_coefficients",
    )(section_steps, tables)
    strips.update(zip(after, send([(None, l) for _, l in after], [edge(strips[(k, None)], l) for k, l in after], None)))

    ncopy = 3 + 3 * nk
    ge = pl.pallas_call(
        functools.partial(assemble_kernel, keys),
        out_shape=shape(3, cxe, cye, cz),
        in_specs=[ANY] + [ANY] * nk,
        out_specs=VM,
        scratch_shapes=[pltpu.VMEM((3, cxe, cye, cz), f32), pltpu.SemaphoreType.DMA((ncopy,))],
        compiler_params=params(10),
        name="assemble",
    )(co, *[strips[k] for k in keys])

    state, handed = None, None
    cbuf = pltpu.VMEM((cxe, cye, cz), f32)
    arrive = straight + [(None, 0)] * (0 in colors(ngy)) + after
    for n in range(nt):
        last = n == nt - 1
        args = [section_steps, ge, coef, co]
        specs = [SM, VM, VM, VM]
        alias = {}
        if n > 0:
            alias = {len(args): 0}
            args += [state] + handed
            specs += [VM] + [ANY] * len(handed)
            if n == 1:
                args.append(arrived)
                specs.append(ANY)
        sent = [] if last else straight
        outs = [shape(3, cx, cy, cz), shape(cx, cy, cz)] + [shape(*dims(k, l, CW, cx, cy)) for k, l in sent]
        ospecs = [VM] * len(outs)
        scratch = [cbuf] * 4 + [pltpu.VMEM((2, cxe, cye, cz), f32), pltpu.SemaphoreType.DMA((nk + 1,))]
        if last:
            args.append(ready)
            specs.append(VM)
            outs.append(shape(3, nx, ny, cz))
            ospecs.append(ANY)
            scratch += [pltpu.VMEM((3, nx, ny, cz), f32), pltpu.SemaphoreType.DMA((PIECES * 3,))]
        res = pl.pallas_call(
            functools.partial(chain_kernel, n, sent, arrive if n else [], last),
            out_shape=outs,
            in_specs=specs,
            out_specs=ospecs,
            scratch_shapes=scratch,
            input_output_aliases=alias,
            compiler_params=params(20 if last else 14),
            name=f"chain_{n}",
        )(*args)
        state = res[0]
        if not last:
            whole = res[1]
            own = lax.ppermute(whole, AXES, routes(sizes, None, None, n))
            moving = [own] + send(straight, res[2:], n)
            if n == nt - 2:
                ready = pl.pallas_call(
                    prepare_kernel,
                    out_shape=shape(3, nx, ny, cz),
                    in_specs=[ANY] + [VM] * 5 + [ANY],
                    out_specs=VM,
                    scratch_shapes=[pltpu.VMEM((nx, ny, cz), f32), pltpu.SemaphoreType.DMA((1,))],
                    compiler_params=params(16),
                    name="prepare",
                )(u, arrived, early, w1, w2, co, whole)
                moving.append(ready)
            moving = lax.optimization_barrier(moving)
            if n == 0:
                late, moving[0] = lax.optimization_barrier((w2, moving[0]))
                early = lax.ppermute(late, "tm", [(0, 1)])
            own, got = moving[0], moving[1 : 1 + len(straight)]
            ready = moving[-1]
            rows = [own] + [got[straight.index((k, None))] for k in colors(ngx)]
            side = []
            for l in colors(ngy)[:1]:
                strip = edge(jnp.concatenate(rows, axis=0), l)
                pairs = [p for p in routes(sizes, None, l, None) if p[1] // (ngx * ngy) == n + 1]
                strip = lax.ppermute(strip, AXES, pairs)
                side = [strip[:cx]] + [strip[cx + i * CW : cx + i * CW + CW] for i in range(len(after))]
            handed = [own] + got + side
    return res[2][None]


def solution(mesh):
    sizes = tuple(mesh.shape[a] for a in AXES)
    return jax.shard_map(
        functools.partial(per_device, sizes),
        mesh=mesh,
        in_specs=(P("tm", None, "gx", "gy", None), P(), P(), P("gx", "gy")),
        out_specs=P("tm", None, "gx", "gy", None),
        check_vma=False,
    )
```

```python
import functools
import jax
import jax.numpy as jnp
from jax import lax
from jax.experimental import pallas as pl
from jax.experimental.pallas import tpu as pltpu
from jax.sharding import PartitionSpec as P

TILE = 4
FW = 8
CW = 6
CN = 3
SUB = 1
FEW, MANY, LOW = 8, 8, 6
YW = 8
STEP_UNIT = 0.05
WEIGHTS = ((5.0 / 24.0, 1.0 / 3.0, -1.0 / 24.0), (-1.0 / 24.0, 1.0 / 3.0, 5.0 / 24.0))
AXES = ("tm", "gx", "gy")
ANY = pl.BlockSpec(memory_space=pl.ANY)
VM = pl.BlockSpec(memory_space=pltpu.VMEM)
SM = pl.BlockSpec(memory_space=pltpu.SMEM)
f32 = jnp.float32


def params(mib):
    return pltpu.CompilerParams(vmem_limit_bytes=mib * 1024 * 1024)


def shape(*dims):
    return jax.ShapeDtypeStruct(dims, f32)


def partner(i, color, size):
    j = i + 1 if (i + color) % 2 == 0 else i - 1
    return j if 0 <= j < size else None


def colors(size):
    return [k for k in (0, 1) if any(partner(i, k, size) is not None for i in range(size))]


def routes(sizes, cx, cy, hop):
    nt, nx, ny = sizes
    out = []
    for t in range(nt):
        if hop is not None and t != hop:
            continue
        for x in range(nx):
            px = x if cx is None else partner(x, cx, nx)
            for y in range(ny):
                py = y if cy is None else partner(y, cy, ny)
                if px is None or py is None:
                    continue
                target = t if hop is None else t + 1
                out.append(((t * nx + px) * ny + py, (target * nx + x) * ny + y))
    return out


def message_keys(nx, ny):
    keys = [(k, None) for k in colors(nx)]
    keys += [(k, l) for k in colors(nx) for l in colors(ny)]
    keys += [(None, l) for l in colors(ny)]
    return keys


def upper(axis, color):
    return lax.rem(lax.axis_index(axis) + color, 2) == 0


def pick(cond, a, b):
    return jnp.where(cond, jnp.int32(a), jnp.int32(b))


def times(steps, sect):
    h = steps[sect].astype(f32) * STEP_UNIT
    return h, 0.5 * h


def reaction(v):
    return v - v * v * v


def run_copies(pairs, sems):
    copies = [pltpu.make_async_copy(a, b, sems.at[i]) for i, (a, b) in enumerate(pairs)]
    for c in copies:
        c.start()
    for c in copies:
        c.wait()


def table_rows(rows, tiles):
    return -(-tiles // rows)


def table_copies(table, msg, base, out):
    tiles, height = table.shape[0], msg.shape[1]
    pairs = []
    for i in range(table_rows(height, tiles)):
        n = min(height, tiles - i * height)
        pair = (table.at[pl.ds(i * height, n)], msg.at[base + i, pl.ds(0, n)])
        pairs.append(pair if out else pair[::-1])
    return pairs


def pack_kernel(keys, u, table, *rest):
    outs, sems = rest[:-1], rest[-1]
    nx, ny = u.shape[1], u.shape[2]
    pairs = []
    for (k, l), o in zip(keys, outs):
        w = nx if k is None else FW
        xs = pl.ds(0 if k is None else pick(upper("gx", k), nx - FW, 0), w)
        ys = pl.ds(0, ny) if l is None else pl.ds(pl.multiple_of(pick(upper("gy", l), ny - YW, 0), 8), YW)
        pairs += [(u.at[j, xs, ys, :], o.at[pl.ds(j * w, w)]) for j in range(3)]
        pairs += table_copies(table, o, 3 * w, True)
    run_copies(pairs, sems)


def permuted(ref, *lead):
    t_count = ref.shape[-2] // 8
    return jnp.concatenate([ref[(*lead, pl.ds(t, 8, stride=t_count))] for t in range(t_count)], axis=-2)


def store_plain(ref, lead, value):
    t_count = value.shape[-2] // 8
    for t in range(t_count):
        ref[(*lead, pl.ds(t, 8, stride=t_count))] = value[..., t * 8 : t * 8 + 8, :]


def expand(tables, tx, ty, row, piece, cells):
    sub = lax.broadcasted_iota(jnp.int32, (8, 128), 0)
    lane = lax.broadcasted_iota(jnp.int32, (8, 128), 1)
    if isinstance(row, int):
        sx = 0 if row < 0 else (2 if row >= tx else 1)
        r = row - (sx - 1) * tx
    else:
        sx = jnp.where(row < 0, 0, jnp.where(row >= tx, 2, 1))
        r = row - (sx - 1) * tx
    runs = ty * cells // 8
    per = 8 // cells
    sy, first = (0, ty - per) if piece < 0 else ((2, 0) if piece >= runs else (1, piece * per))
    hot = lane == first + lax.div(sub, cells)
    return jnp.sum(jnp.where(hot, tables[sx, sy, pl.ds(r, 1), :], 0.0), axis=1, keepdims=True)


def fill_coefficients(tables, local, cells, low, rows, plain, write):
    tx, ty = local
    count = plain.shape[1] // 8
    for i in range(rows):
        slot = i % plain.shape[0]
        for p in range(count):
            k = expand(tables, tx, ty, low + i, p - 1, cells)
            plain[slot, p * 8 : p * 8 + 8, :] = jnp.broadcast_to(k, (8, 128))
        write(i, jnp.concatenate([plain[slot, pl.ds(t, 8, stride=count), :] for t in range(count)], axis=0))


def coarse_coefficient_kernel(local, steps, tables, coarse, plain):
    _, a = times(steps, lax.axis_index("tm"))

    def write(i, k):
        inv = 1.0 / (1.0 + a * k * 3.0)
        coarse[0, i] = a * k * inv
        coarse[1, i] = inv

    rows = local[0] + CW
    fill_coefficients(tables, local, TILE // 2, -(CW // 2), rows, plain, write)
    for i in range(rows, coarse.shape[1]):
        write(i, jnp.zeros(plain.shape[1:], f32))


def neighbours(v, masks):
    c = v[1:-1]
    px = v[2:] + v[:-2]
    before = jnp.concatenate([pltpu.roll(c[:, -8:], 1, 1), c[:, :-8]], axis=1)
    after = jnp.concatenate([c[:, 8:], pltpu.roll(c[:, :8], 7, 1)], axis=1)
    z = pltpu.roll(c, 1, 2) * masks[0] + pltpu.roll(c, 127, 2) * masks[1]
    return c, px + (before + after), z


def z_masks():
    lane = lax.broadcasted_iota(jnp.int32, (1, 8, 128), 2)
    return (jnp.where(lane == 0, 0.0, 1.0), jnp.where(lane == 127, 0.0, 1.0))


def wide_masks(rows, y):
    return tuple(jnp.concatenate([jnp.concatenate([m] * (y // 8), axis=1)] * rows, axis=0) for m in z_masks())


def sweep_rows(own, width, r, step, body):
    gx, ngx = lax.axis_index("gx"), lax.axis_size("gx")
    n = own + r * min(ngx - 1, 2)
    pad = -n % step
    if ngx == 2:
        begin = width - pick(gx > 0, r, pad)
    else:
        begin = width - r * min(ngx - 1, 2) // 2
    lax.fori_loop(0, (n + pad) // step, lambda i, _: (body(begin + i * step), 0)[1], 0)


def clear_walls(width, own, bufs, count=CW):
    gx, ngx = lax.axis_index("gx"), lax.axis_size("gx")
    for b in bufs:
        zero = jnp.zeros((count,) + b.shape[1:], f32)

        @pl.when(gx == 0)
        def _():
            b[width - count : width] = zero

        @pl.when(gx == ngx - 1)
        def _():
            b[width + own : width + own + count] = zero


SEAM = 12
FIELDS = 10


class Stages:
    def __init__(self, u, f0, q0, qa, qb, p2, w1, w2, fine, h, a, tile_of):
        self.u, self.f0, self.q0, self.qa, self.qb, self.p2, self.w1, self.w2 = u, f0, q0, qa, qb, p2, w1, w2
        self.fine, self.h, self.a, self.tile_of = fine, h, a, tile_of

    def coef(self, n, x, step):
        return jnp.stack([self.fine[n, self.tile_of(x + i)] for i in range(step)])

    def forces(self, x, step, masks):
        k, h, a = self.coef(0, x, step), self.h, self.a
        c, f = [], []
        for j in range(3):
            cj, pj, zj = neighbours(self.u(j, pl.ds(x - 1, step + 2)), masks)
            c.append(cj)
            f.append(reaction(cj) + k * (pj + zj - 6.0 * cj))
        at = pl.ds(x, step)
        self.f0[at] = f[0]
        h0 = WEIGHTS[0][0] * f[0] + WEIGHTS[0][1] * f[1] + WEIGHTS[0][2] * f[2]
        h1 = WEIGHTS[1][0] * f[0] + WEIGHTS[1][1] * f[1] + WEIGHTS[1][2] * f[2]
        self.q0[at] = (c[0] + h * h0 - c[1]) * self.coef(2, x, step)
        self.p2[at] = h * h1 - c[2] - a * reaction(c[1])

    def jacobi(self, src, start, x, step, masks):
        _, p, z = neighbours(src[pl.ds(x - 1, step + 2)], masks)
        return start[pl.ds(x, step)] + self.coef(1, x, step) * (p + z)

    def into(self, dst, src, start):
        def body(x, step, masks):
            dst[pl.ds(x, step)] = self.jacobi(src, start, x, step, masks)
        return body

    def end1(self, x, step, masks):
        at = pl.ds(x, step)
        w = self.u(1, at) + self.jacobi(self.qb, self.q0, x, step, masks)
        self.w1[at] = w
        self.p2[at] = (w + self.a * reaction(w) + self.p2[at]) * self.coef(2, x, step)

    def end2(self, x, step, masks):
        at = pl.ds(x, step)
        self.w2[at] = self.u(2, at) + self.jacobi(self.qb, self.p2, x, step, masks)

    def bodies(self):
        return [
            (1, self.forces),
            (2, self.into(self.qa, self.q0, self.q0)),
            (3, self.into(self.qb, self.qa, self.q0)),
            (4, self.end1),
            (5, self.into(self.qa, self.p2, self.p2)),
            (6, self.into(self.qb, self.qa, self.p2)),
            (7, self.end2),
        ]

    def coarse_pair(self, x, i, w1o, w2o, co, plain, tmp, ny, turn=0):
        ye = ny + 2 * YW
        masks = wide_masks(2, ye)
        h, a = self.h, self.a

        def pair_sum(v):
            v = v[0] + v[1]
            return jnp.concatenate([v[t : t + 8] + v[t + 8 : t + 16] for t in range(0, ye, 16)], axis=0)

        at = pl.ds(x, 2)
        k = self.coef(0, x, 2)
        g = [self.f0[at]]
        w = [self.u(0, at)]
        for m, (ref, out) in enumerate(((self.w1, w1o), (self.w2, w2o))):
            c, p, z = neighbours(ref[pl.ds(x - 1, 4)], masks)
            w.append(c)
            g.append(reaction(c) + k * (p + z - 6.0 * c))
            slot = 4 * turn + 2 * m
            store_plain(tmp, (slot,), c[0])
            store_plain(tmp, (slot + 1,), c[1])
            out[pl.ds(2 * i, 2)] = tmp[slot : slot + 2, YW : YW + ny]
        c0, c1 = [pair_sum(wt[0] * g[0] + wt[1] * g[1] + wt[2] * g[2]) * 0.25 for wt in WEIGHTS]
        u0, u1, u2 = [pair_sum(v) * 0.25 for v in w]
        start = jnp.where(lax.axis_index("tm") == 0, u0 + a * reaction(u0), 0.0)
        values = (start + h * c0 - a * reaction(u0) - u1, u1, h * c1 - a * reaction(u1) - u2, u0, u2)
        for n, v in enumerate(values):
            store_plain(plain, (5 * turn + n,), v)
            co[n, i] = plain[5 * turn + n, YW // 2 : YW // 2 + ny // 2]


def parts(body, step, masks, x):
    for i in range(0, step, SUB):
        body(x + i, SUB, masks)


def seam_count(size):
    return min(size - 1, 2)


def seam_is_low(seam):
    return lax.axis_index("gx") > 0 if lax.axis_size("gx") == 2 else seam == 0


def target_y(l, ny):
    return pl.ds(YW, ny) if l is None else pl.ds(pl.multiple_of(pick(upper("gy", l), YW + ny, 0), 8), YW)


def inner_kernel(keys, local, seams, steps, u, table, *rest):
    nmsg = len(keys)
    msgs, rest = rest[:nmsg], rest[nmsg:]
    w1o, w2o, co, seam, rest = rest[0], rest[1], rest[2], rest[3], rest[4:]
    ue, f0, q0, qa, qb, p2, w1, w2, fine, tables, plain, tmp, sems = rest
    nx, ny = u.shape[1], u.shape[2]
    ye = ny + 2 * YW
    h, a = times(steps, lax.axis_index("tm"))

    if nmsg < 2:
        def clear(i, _):
            for j in range(3):
                ue[j, i] = jnp.zeros((ye, 128), f32)
            return 0
        lax.fori_loop(0, ue.shape[1], clear, 0)
    clear_walls(FW, nx, [ue.at[0], ue.at[1], ue.at[2], q0, qa, qb, p2, w1, w2], FW)
    for j in (0, 2):
        tables[1, j] = jnp.zeros(tables.shape[2:], f32)
    pairs = [(u, ue.at[:, pl.ds(FW, nx), pl.ds(YW, ny), :])]
    for (_, l), m in zip(keys, msgs):
        pairs += [(m.at[pl.ds(j * nx, nx)], ue.at[j, pl.ds(FW, nx), target_y(l, ny), :]) for j in range(3)]
        pairs += table_copies(tables.at[1, pick(upper("gy", l), 2, 0)], m, 3 * nx, False)
    pairs.append((table, tables.at[1, 1]))
    run_copies(pairs, sems)

    def write(i, k):
        inv = 1.0 / (1.0 + a * k * 6.0)
        fine[0, i] = k
        fine[1, i] = a * k * inv
        fine[2, i] = inv

    ft = FW // TILE
    for i in list(range(ft)) + list(range(ft + local[0], fine.shape[1])):
        write(i, jnp.zeros((ye, 128), f32))
    fill_coefficients(tables, local, TILE, 0, local[0], tmp, lambda i, k: write(ft + i, k))
    st = Stages(
        lambda j, at: permuted(ue, j, at), f0, q0, qa, qb, p2, w1, w2, fine, h, a, lambda x: lax.div(x, TILE)
    )
    for k, body in st.bodies():
        n = nx - k * seams
        step = min((s for s in range(7, 33) if seams < 2 or n % s == 0), key=lambda s: (-n % s, -s), default=2)
        sweep_rows(nx, FW, -k, step, functools.partial(parts, body, step, wide_masks(SUB, ye)))

    def coarse_rows(x):
        for turn in range(2):
            y = x + 2 * turn
            st.coarse_pair(y, lax.div(y - FW, 2), w1o, w2o, co, plain, tmp, ny, turn)

    sweep_rows(nx, FW, -8, 4, coarse_rows)
    for n in range(seams):
        low = seam_is_low(n)
        src, dst = pick(low, FW, FW + nx - SEAM), pick(low, FW, 0)

        def keep(i, _):
            x, to = pl.ds(src + 4 * i, 4), pl.ds(dst + 4 * i, 4)
            for j in range(3):
                seam[n, j, to] = permuted(ue, j, x)
            for j, b in enumerate((f0, q0, qa, qb, p2, w1, w2)):
                seam[n, 3 + j, to] = b[x]
            return 0

        lax.fori_loop(0, SEAM // 4, keep, 0)


def seam_kernel(keys, ckeys, local, seams, steps, table, *rest):
    nmsg = len(keys)
    msgs, rest = rest[:nmsg], rest[nmsg + 4 :]
    w1o, w2o, co, seam, tables = rest[:5]
    nc = len(ckeys)
    couts, rest = rest[5 : 5 + nc], rest[5 + nc :]
    halo, fine, plain, tmp, sems = rest
    nx, ny = w1o.shape[0], w1o.shape[1]
    ye = ny + 2 * YW
    h, a = times(steps, lax.axis_index("tm"))
    for i in range(3):
        for j in range(3):
            if (i, j) != (1, 1):
                tables[i, j] = jnp.zeros(tables.shape[2:], f32)
    if len(colors(lax.axis_size("gy"))) < 2 or len(colors(lax.axis_size("gx"))) < min(seams, 2):
        halo[...] = jnp.zeros(halo.shape, f32)
    pairs = []
    for (k, l), m in zip(keys, msgs):
        w = nx if k is None else FW
        if k is not None:
            n = 0 if seams == 1 else pick(upper("gx", k), 1, 0)
            pairs += [(m.at[pl.ds(j * w, w)], halo.at[n, j, :, target_y(l, ny), :]) for j in range(3)]
        sx = 1 if k is None else pick(upper("gx", k), 2, 0)
        sy = 1 if l is None else pick(upper("gy", l), 2, 0)
        pairs += table_copies(tables.at[sx, sy], m, 3 * w, False)
    pairs.append((table, tables.at[1, 1]))
    run_copies(pairs, sems)
    tx = local[0]
    for n in range(seams):
        low = seam_is_low(n)

        def write(i, k):
            inv = 1.0 / (1.0 + a * k * 6.0)
            fine[0, i] = k
            fine[1, i] = a * k * inv
            fine[2, i] = inv

        fill_coefficients(
            tables, local, TILE, pick(low, -(FW // TILE), tx - SEAM // TILE), fine.shape[1], tmp, write
        )
        to = pick(low, 0, SEAM)
        for i in range(0, FW, 4):
            for j in range(3):
                seam[n, j, pl.ds(to + i, 4)] = permuted(halo, n, j, pl.ds(i, 4))
        st = Stages(
            lambda j, at: seam[n, j, at], *[seam.at[n, 3 + j] for j in range(7)], fine, h, a, lambda x: lax.div(x, TILE)
        )
        for k, body in st.bodies():
            step = FEW if k == 1 else MANY
            masks = wide_masks(SUB, ye)
            first = pick(low, k, SEAM - k)
            lax.fori_loop(0, 8 // step, lambda i, _: (parts(body, step, masks, first + i * step), 0)[1], 0)
        first = pick(low, FW, SEAM - 8)
        row = pick(low, 0, nx // 2 - 4)
        for i in range(4):
            st.coarse_pair(first + 2 * i, row + i, w1o, w2o, co, plain, tmp, ny, i % 2)
    cx, cy = nx // 2, ny // 2
    fields = ((0, CW), (1, CN), (2, CN))
    for (k, l), o in zip(ckeys, couts):
        ys = pl.ds(0, cy) if l is None else pl.ds(pl.multiple_of(pick(upper("gy", l), cy - YW, 0), 8), YW)
        at = 0
        for fld, width in fields:
            if k is None:
                width, first = cx, 0
            else:
                first = pick(upper("gx", k), cx - width, 0)
            o[pl.ds(at, width)] = co[fld, pl.ds(first, width), ys, :]
            at += width


def assemble_kernel(keys, co, *rest):
    nm = len(keys)
    msgs, (gp, ge), sems = rest[:nm], rest[nm : nm + 2], rest[nm + 2]
    cx, cy = co.shape[1], co.shape[2]

    def clear(i):
        for f in range(3):
            ge[f, i] = jnp.zeros(ge.shape[2:], f32)

    for i in (*range(CW), *range(CW + cx, ge.shape[1])):
        clear(i)
    if len(colors(lax.axis_size("gy"))) < 2:
        for i in range(CW, CW + cx):
            clear(i)
    fields = ((0, CW), (1, CN), (2, CN))
    pairs = []

    for f, _ in fields:
        pairs.append((co.at[f], ge.at[f].at[pl.ds(CW, cx), pl.ds(YW, cy), :]))
    for (k, l), m in zip(keys, msgs):
        ys = pl.ds(YW, cy) if l is None else pl.ds(pl.multiple_of(pick(upper("gy", l), YW + cy, 0), 8), YW)
        at = 0
        for f, width in fields:
            if k is None:
                width, first = cx, CW
            else:
                first = pick(upper("gx", k), CW + cx, CW - width)
            pairs.append((m.at[pl.ds(at, width)], ge.at[f].at[pl.ds(first, width), ys, :]))
            at += width
    run_copies(pairs, sems)

    def order(i, _):
        at = pl.ds(8 * i, 8)
        for f in range(3):
            gp[f, at] = permuted(ge, f, at)
        return 0

    lax.fori_loop(0, ge.shape[1] // 8, order, 0)
    for x in range(ge.shape[1] // 8 * 8, ge.shape[1]):
        for f in range(3):
            gp[f, pl.ds(x, 1)] = permuted(ge, f, pl.ds(x, 1))


def chain_kernel(turn, keys, arrive, last, steps, ge, coef, co, *rest):
    first = turn == 0
    if not first:
        _, own, rest = rest[0], rest[1], rest[2:]
        nm = len(arrive)
        msgs, rest = rest[:nm], rest[nm:]
        if turn == 1:
            rest = rest[1:]
        if last:
            ready, rest = rest[0], rest[1:]
    state = rest[0]
    rest = rest[1:]
    no = len(keys)
    whole, couts, rest = rest[0], rest[1 : 1 + no], rest[1 + no :]
    if last:
        final, stage, finals = rest[0], rest[-2], rest[-1]
        rest = rest[1:-2]
    cin, q0, qa, qb, plain, sems = rest
    cx, cy = co.shape[1], co.shape[2]
    ye = cy + 2 * YW
    sect = lax.axis_index("tm")
    h, a = times(steps, sect)
    ngx, ngy = lax.axis_size("gx"), lax.axis_size("gy")

    step = 1
    masks = wide_masks(step, ye)

    def rows(r, body):
        n = cx + r * min(ngx - 1, 2)
        sweep_rows(cx, CW, r, n, lambda x: [body(x + i) for i in range(0, n, step)])

    def coefs(n, x):
        return jnp.stack([coef[n, lax.div(x + i, 2)] for i in range(step)])

    def jacobi(src, x):
        _, p, z = neighbours(src[pl.ds(x - 1, step + 2)], masks)
        return q0[pl.ds(x, step)] + coefs(0, x) * (0.25 * p + z)

    def into(dst, src):
        def body(x):
            dst[pl.ds(x, step)] = jacobi(src, x)
        return body

    def start(x):
        at = pl.ds(x, step)
        r = ge[0, at]
        if not first:
            v = permuted(cin, at)
            r = v + a * reaction(v) + r
        q0[at] = r * coefs(1, x)

    def keep(m, value):
        for i in range(0, cx, 4):
            state[m, i : i + 4] = value(slice(CW + i, CW + i + 4), slice(i, i + 4))

    @pl.when(sect == turn)
    def _():
        clear_walls(CW, cx, (q0, qa, qb))
        if not first:
            if len(colors(ngy)) < 2:
                cin[...] = jnp.zeros(cin.shape, f32)
            else:
                clear_walls(CW, cx, (cin,))
            pairs = [(own, cin.at[pl.ds(CW, cx), pl.ds(YW, cy), :])]
            for (k, l), m in zip(arrive, msgs):
                if k is None:
                    xs = pl.ds(CW, cx)
                else:
                    xs = pl.ds(pick(upper("gx", k), CW + cx, 0), CW)
                ys = pl.ds(YW, cy) if l is None else pl.ds(pl.multiple_of(pick(upper("gy", l), YW + cy, 0), 8), YW)
                pairs.append((m, cin.at[xs, ys, :]))
            run_copies(pairs, sems)
        rows(6, start)
        rows(5, into(qa, q0))
        rows(4, into(qb, qa))

        def middle(x):
            at = pl.ds(x, step)
            w = ge[1, at] + jacobi(qb, x)
            q0[at] = (w + a * reaction(w) + ge[2, at]) * coefs(1, x)
            store_plain(plain, (0, at), w)

        rows(3, middle)
        keep(0, lambda x, at: co[3, at] if first else cin[x, YW : YW + cy])
        keep(1, lambda x, at: plain[0, x, YW : YW + cy])

    copies = correct((0, 1), ready, state, final, stage, finals) if last else []

    @pl.when(sect == turn)
    def _():
        rows(2, into(qa, q0))
        rows(1, into(qb, qa))

        def end(x):
            store_plain(plain, (1, pl.ds(x, step)), jacobi(qb, x))

        rows(0, end)

        def value(x, at):
            v = co[4, at] + plain[1, x, YW : YW + cy]
            whole[at] = v
            return v

        keep(2, value)
        for (k, l), o in zip(keys, couts):
            xs = pl.ds(0, cx) if k is None else pl.ds(pick(upper("gx", k), cx - CW, 0), CW)
            ys = pl.ds(0, cy) if l is None else pl.ds(pl.multiple_of(pick(upper("gy", l), cy - YW, 0), 8), YW)
            o[...] = state[2, xs, ys, :]

    if last:
        for c in copies + correct((2,), ready, state, final, stage, finals):
            c.wait()


PIECES = 4


def prepare_kernel(u, arrived, early, w1, w2, co, _, ready, u0, sems):
    run_copies([(u.at[0], u0)], sems)
    sect = lax.axis_index("tm")
    ny = u0.shape[1]
    ft, ct = ny // 8, ny // 16

    def row(i, _):
        at = pl.ds(2 * i, 2)

        def fine_tile(ref, t):
            return ref[at, pl.ds(t, 8, stride=ft), :]

        for t in range(ct):
            base = []
            for d in range(2):
                came = jnp.where(sect == 1, fine_tile(early, 2 * t + d), fine_tile(arrived, 2 * t + d))
                base.append(jnp.where(sect == 0, fine_tile(u0, 2 * t + d), came))
            both = base[0] + base[1]
            less = ((both[0] + both[1]) * 0.25,) + tuple(co[n, i, pl.ds(t, 8, stride=ct), :] for n in (1, 4))
            for d in range(2):
                to = pl.ds(2 * t + d, 8, stride=ft)
                ready[0, at, to, :] = base[d] - less[0]
                ready[1, at, to, :] = fine_tile(w1, 2 * t + d) - less[1]
                ready[2, at, to, :] = fine_tile(w2, 2 * t + d) - less[2]
        return 0

    lax.fori_loop(0, u0.shape[0] // 2, row, 0)


def correct(nodes, ready, state, out, stage, sems):
    nx, ny = ready.shape[1], ready.shape[2]
    rows = nx // PIECES
    copies = []
    for m in nodes:
        for p in range(PIECES):
            mine = range(p * rows // 2, (p + 1) * rows // 2)
            for i in mine:
                c = state[m, i]
                for d in range(2):
                    stage[m, 2 * i, pl.ds(d, ny // 2, stride=2), :] = c
            for i in mine:
                c = stage[m, 2 * i]
                for d in range(2):
                    stage[m, 2 * i + d] = ready[m, 2 * i + d] + c
            part = pl.ds(p * rows, rows)
            copies.append(pltpu.make_async_copy(stage.at[m, part], out.at[m, part], sems.at[m * PIECES + p]))
            copies[-1].start()
    return copies


def per_device(sizes, fine_nodes, section_steps, diffusivities, tile_kinds):
    nt, ngx, ngy = sizes
    u = fine_nodes[0]
    nodes, nx, ny, cz = u.shape
    cx, cy = nx // 2, ny // 2
    keys = message_keys(ngx, ngy)
    nk = len(keys)

    def dims(k, l, wx, lx, ly):
        return (lx if k is None else wx, ly if l is None else YW, cz)

    def send(some, arrays, hop):
        return [lax.ppermute(v, AXES, routes(sizes, k, l, hop)) for (k, l), v in zip(some, arrays)]

    def edge(v, l):
        first = jnp.where(upper("gy", l), v.shape[-2] - YW, 0)
        return lax.dynamic_slice_in_dim(v, first, YW, axis=v.ndim - 2)

    now = [(k, l) for k, l in keys if k is None or l != 0]
    after = [(k, l) for k, l in keys if k is not None and l == 0]
    straight = [(k, l) for k, l in now if l != 0]

    picks = tile_kinds[:, :, None] == jnp.arange(diffusivities.shape[0], dtype=jnp.int32)
    table = jnp.sum(jnp.where(picks, diffusivities, 0.0), axis=-1)
    local = table.shape
    table = jnp.pad(table, ((0, -local[0] % 8), (0, 128 - local[1])))
    tp = table.shape[0]

    def fine_dims(k, l):
        a, b, c = dims(k, l, FW, nx, ny)
        return shape(nodes * a + table_rows(b, tp), b, c)

    packed = pl.pallas_call(
        functools.partial(pack_kernel, keys),
        out_shape=[fine_dims(k, l) for k, l in keys],
        in_specs=[ANY, ANY],
        out_specs=[ANY] * nk,
        scratch_shapes=[pltpu.SemaphoreType.DMA((nk * (3 + tp),))],
        compiler_params=params(4),
        name="pack",
    )(u, table)
    halos = send(keys, packed, None)

    fye, cye, cxe = ny + 2 * YW, cy + 2 * YW, cx + 2 * CW + 4
    xe = nx + 2 * FW
    buf = pltpu.VMEM((xe, fye, cz), f32)
    depth = CW + 2 * CN
    seams = seam_count(ngx)
    ykeys = [key for key in keys if key[0] is None]
    yhalos = [m for key, m in zip(keys, halos) if key[0] is None]
    inner = pl.pallas_call(
        functools.partial(inner_kernel, ykeys, local, seams),
        out_shape=[
            shape(nx, ny, cz), shape(nx, ny, cz), shape(5, cx, cy, cz), shape(seams, FIELDS, FW + SEAM, fye, cz)
        ],
        in_specs=[SM, ANY, ANY] + [ANY] * len(ykeys),
        out_specs=[VM] * 4,
        scratch_shapes=[pltpu.VMEM((3, xe, fye, cz), f32)] + [buf] * 7
        + [
            pltpu.VMEM((3, xe // TILE, fye, cz), f32),
            pltpu.VMEM((3, 3, tp, cz), f32),
            pltpu.VMEM((10, fye // 2, cz), f32),
            pltpu.VMEM((8, fye, cz), f32),
            pltpu.SemaphoreType.DMA((nk * (3 + tp) + 2,)),
        ],
        compiler_params=params(38),
        cost_estimate=pl.CostEstimate(flops=200 * nx * ny * cz, bytes_accessed=40_000_000, transcendentals=0),
        name="fine_inner",
    )(section_steps, u, table, *yhalos)
    out = pl.pallas_call(
        functools.partial(seam_kernel, keys, now, local, seams),
        out_shape=[shape(*v.shape) for v in inner] + [shape(3, 3, tp, cz)]
        + [shape(*dims(k, l, depth, 3 * cx, cy)) for k, l in now],
        in_specs=[SM, ANY] + [ANY] * nk + [VM] * 4,
        out_specs=[VM] * (5 + len(now)),
        scratch_shapes=[
            pltpu.VMEM((seams, 3, FW, fye, cz), f32),
            pltpu.VMEM((3, (FW + SEAM) // TILE, fye, cz), f32),
            pltpu.VMEM((10, fye // 2, cz), f32),
            pltpu.VMEM((8, fye, cz), f32),
            pltpu.SemaphoreType.DMA((nk * (3 + tp) + 2,)),
        ],
        input_output_aliases={2 + nk + i: i for i in range(4)},
        compiler_params=params(24),
        name="fine_seam",
    )(section_steps, table, *halos, *inner)
    w1, w2, co, _, tables = out[:5]
    strips = dict(zip(now, lax.optimization_barrier(send(now, out[5:], None))))
    arrived = lax.ppermute(w2, "tm", [(i, i + 1) for i in range(1, nt - 1)])
    coef = pl.pallas_call(
        functools.partial(coarse_coefficient_kernel, local),
        out_shape=shape(2, cxe // 2, cye, cz),
        in_specs=[SM, VM],
        out_specs=VM,
        scratch_shapes=[pltpu.VMEM((4, cye, cz), f32)],
        compiler_params=params(4),
        name="coarse_coefficients",
    )(section_steps, tables)
    strips.update(zip(after, send([(None, l) for _, l in after], [edge(strips[(k, None)], l) for k, l in after], None)))

    ncopy = 3 + 3 * nk
    ge = pl.pallas_call(
        functools.partial(assemble_kernel, keys),
        out_shape=shape(3, cxe, cye, cz),
        in_specs=[ANY] + [ANY] * nk,
        out_specs=VM,
        scratch_shapes=[pltpu.VMEM((3, cxe, cye, cz), f32), pltpu.SemaphoreType.DMA((ncopy,))],
        compiler_params=params(10),
        name="assemble",
    )(co, *[strips[k] for k in keys])

    state, handed = None, None
    cbuf = pltpu.VMEM((cxe, cye, cz), f32)
    arrive = straight + [(None, 0)] * (0 in colors(ngy)) + after
    for n in range(nt):
        last = n == nt - 1
        args = [section_steps, ge, coef, co]
        specs = [SM, VM, VM, VM]
        alias = {}
        if n > 0:
            alias = {len(args): 0}
            args += [state] + handed
            specs += [VM] + [ANY] * len(handed)
            if n == 1:
                args.append(arrived)
                specs.append(ANY)
        sent = [] if last else straight
        outs = [shape(3, cx, cy, cz), shape(cx, cy, cz)] + [shape(*dims(k, l, CW, cx, cy)) for k, l in sent]
        ospecs = [VM] * len(outs)
        scratch = [cbuf] * 4 + [pltpu.VMEM((2, cxe, cye, cz), f32), pltpu.SemaphoreType.DMA((nk + 1,))]
        if last:
            args.append(ready)
            specs.append(VM)
            outs.append(shape(3, nx, ny, cz))
            ospecs.append(ANY)
            scratch += [pltpu.VMEM((3, nx, ny, cz), f32), pltpu.SemaphoreType.DMA((PIECES * 3,))]
        res = pl.pallas_call(
            functools.partial(chain_kernel, n, sent, arrive if n else [], last),
            out_shape=outs,
            in_specs=specs,
            out_specs=ospecs,
            scratch_shapes=scratch,
            input_output_aliases=alias,
            compiler_params=params(20 if last else 14),
            name=f"chain_{n}",
        )(*args)
        state = res[0]
        if not last:
            whole = res[1]
            own = lax.ppermute(whole, AXES, routes(sizes, None, None, n))
            moving = [own] + send(straight, res[2:], n)
            if n == nt - 2:
                ready = pl.pallas_call(
                    prepare_kernel,
                    out_shape=shape(3, nx, ny, cz),
                    in_specs=[ANY] + [VM] * 5 + [ANY],
                    out_specs=VM,
                    scratch_shapes=[pltpu.VMEM((nx, ny, cz), f32), pltpu.SemaphoreType.DMA((1,))],
                    compiler_params=params(16),
                    name="prepare",
                )(u, arrived, early, w1, w2, co, whole)
                moving.append(ready)
            moving = lax.optimization_barrier(moving)
            if n == 0:
                late, moving[0] = lax.optimization_barrier((w2, moving[0]))
                early = lax.ppermute(late, "tm", [(0, 1)])
            own, got = moving[0], moving[1 : 1 + len(straight)]
            ready = moving[-1]
            rows = [own] + [got[straight.index((k, None))] for k in colors(ngx)]
            side = []
            for l in colors(ngy)[:1]:
                strip = edge(jnp.concatenate(rows, axis=0), l)
                pairs = [p for p in routes(sizes, None, l, None) if p[1] // (ngx * ngy) == n + 1]
                strip = lax.ppermute(strip, AXES, pairs)
                side = [strip[:cx]] + [strip[cx + i * CW : cx + i * CW + CW] for i in range(len(after))]
            handed = [own] + got + side
    return res[2][None]


def solution(mesh):
    sizes = tuple(mesh.shape[a] for a in AXES)
    return jax.shard_map(
        functools.partial(per_device, sizes),
        mesh=mesh,
        in_specs=(P("tm", None, "gx", "gy", None), P(), P(), P("gx", "gy")),
        out_specs=P("tm", None, "gx", "gy", None),
        check_vma=False,
    )
```
